128 devices in a mesh: prow: 8 (over z, core), pcol: 16 (over y, x).
Axes of the slice: x: 4, y: 4, z: 4, core: 2. Of those that a mesh axis runs over, the one named last changes fastest.
Arguments:
- grad_trailing: float32 [8, 8, 256, 4, 16, 256], P(None, 'prow', None, None, 'pcol'), may hold values from -1 to 1, as said below
- panel_one: float32 [8, 8, 256, 256], P(None, 'prow'), may hold values from -6 to 6
- panel_two: float32 [8, 8, 256, 256], P(None, 'prow'), may hold values from -6 to 6
- grad_one: float32 [8, 8, 256, 256], P(None, 'prow'), may hold values from -6 to 6
- grad_two: float32 [8, 8, 256, 256], P(None, 'prow'), may hold values from -6 to 6
- inv_one: float32 [256, 256], replicated, may hold values from -2 to 2, as said below
- inv_two: float32 [256, 256], replicated, may hold values from -2 to 2, as said below
Outputs:
- grad_cols_one: float32 [8, 8, 256, 256], P(None, 'prow')
- grad_cols_two: float32 [8, 8, 256, 256], P(None, 'prow')
- grad_diag_one: float32 [256, 256], replicated
- grad_diag_two: float32 [256, 256], replicated
The draws below stay inside these ranges and needn't reach their ends.
Inputs may be any that keep to these rules, and one draw needn't show every extreme that they name: `grad_trailing`: G is symmetric: the entry at matrix position (a, b) equals the one at (b, a). `inv_one`: lower triangular; the diagonal lies between 0.8 and 1.6. `inv_two`: lower triangular; the diagonal lies between 0.8 and 1.6.
All inputs are finite; a program needn't handle non-finite values.
Results may differ from the reference program's by a relative error of at most 0.000076.
Values sent between devices are 32-bit elements; how exact they have to be, the bound alone decides.
A program may use at most 128 MiB of HBM per device.

```python
import math
import jax
import jax.numpy as jnp
from jax import lax

B = 256
N = 16384
RT = 8
CT = 4
N_PROW = 8
N_PCOL = 16


def draw_grad_trailing(key, part):
    key_base = jax.random.fold_in(key, 3)
    key_one = jax.random.fold_in(key_base, 0)
    entries = jax.random.normal(key_one, (N, N), jnp.float32)
    symmetric = (entries + entries.T) * 0.5 ** 0.5 / math.sqrt(N)
    return symmetric.reshape(RT, N_PROW, B, CT, N_PCOL, B)


def triangle(key):
    key_one, key_two = jax.random.split(key)
    lower_part = jax.random.normal(key_one, (B, B), jnp.float32) * 0.7 / math.sqrt(B)
    diagonal = jax.random.uniform(key_two, (B,), jnp.float32, 0.8, 1.6)
    row_ids = lax.broadcasted_iota(jnp.int32, (B, B), 0)
    col_ids = lax.broadcasted_iota(jnp.int32, (B, B), 1)
    return jnp.where(row_ids > col_ids, lower_part, 0.0) + jnp.where(row_ids == col_ids, diagonal[:, None], 0.0)


def draw_inv_one(key, part):
    return triangle(jax.random.fold_in(key, 1))


def draw_inv_two(key, part):
    return triangle(jax.random.fold_in(key, 2))


def steps_of(own_key, dims, cuts, low, largest):
    def one(axis_at, parts):
        draws = jax.random.uniform(jax.random.fold_in(jax.random.fold_in(own_key, 6), axis_at), (parts,), jnp.float32, low / len(cuts), largest / len(cuts))
        return jnp.repeat(jnp.exp(draws), dims[axis_at] // parts).reshape((-1,) + (1,) * (len(dims) - axis_at - 1))

    factor_of = one(*cuts[0])
    for cut in cuts[1:]:
        factor_of = factor_of * one(*cut)
    return factor_of


def gaussian(rng, extent, scale, reach, shards=(), held_as=jnp.bfloat16):
    result = jax.random.normal(rng, extent, jnp.float32) * scale
    if len(shards) > 0:
        result = steps_of(rng, extent, shards, -0.22, 0.18) * result
    return jnp.clip(result, min=-reach, max=reach).astype(held_as)


def setup_inputs(seed: int = 0) -> dict:
    arg_keys = jax.random.split(jax.random.key(seed), 8)
    return {
        "grad_trailing": draw_grad_trailing(jax.random.fold_in(arg_keys[7], 71), 0),
        "panel_one": gaussian(arg_keys[1], (RT, N_PROW, B, B), 1.0, 6.0, ((1, 8),), jnp.float32),
        "panel_two": gaussian(arg_keys[2], (RT, N_PROW, B, B), 1.0, 6.0, ((1, 8),), jnp.float32),
        "grad_one": gaussian(arg_keys[3], (RT, N_PROW, B, B), 1.0, 6.0, ((1, 8),), jnp.float32),
        "grad_two": gaussian(arg_keys[4], (RT, N_PROW, B, B), 1.0, 6.0, ((1, 8),), jnp.float32),
        "inv_one": draw_inv_one(jax.random.fold_in(arg_keys[7], 71), 0),
        "inv_two": draw_inv_two(jax.random.fold_in(arg_keys[7], 71), 0),
    }


def matmul(left, right):
    return jnp.dot(left, right, precision=lax.Precision.HIGHEST, preferred_element_type=jnp.float32)

def reference(grad_trailing, panel_one, panel_two, grad_one, grad_two, inv_one, inv_two):
    norm_scale = 1.0 / math.sqrt(N)
    trailing = grad_trailing.reshape(N, N)
    lower_one = panel_one.reshape(N, B)
    lower_two = panel_two.reshape(N, B)
    upstream_one = grad_one.reshape(N, B)
    upstream_two = grad_two.reshape(N, B)
    prod_two = matmul(trailing, lower_two)
    cols_two = matmul(upstream_two - 2.0 * prod_two, inv_two)
    diag_two = -norm_scale * matmul(cols_two.T, lower_two)
    cross_block = norm_scale * matmul(cols_two.T, lower_one)
    prod_one = matmul(trailing, lower_one)
    corner = lower_one[:B]
    resid_one = upstream_one - 2.0 * prod_one - norm_scale * matmul(cols_two, corner)
    resid_one = resid_one.at[:B].add(-cross_block)
    cols_one = matmul(resid_one, inv_one)
    diag_one = -norm_scale * matmul(cols_one.T, lower_one)
    return (cols_one.reshape(RT, N_PROW, B, B), cols_two.reshape(RT, N_PROW, B, B), diag_one, diag_two)
```

```python
import math

import jax
import jax.numpy as jnp
from jax import lax
from jax.experimental import pallas as pl
from jax.experimental.pallas import tpu as pltpu
from jax.sharding import PartitionSpec as P

N = 16384
B = 256
HALF = B // 2
QUARTER = B // 4
SCALE = 1.0 / math.sqrt(N)
F32 = jnp.float32
BF16 = jnp.bfloat16

CHILDREN = (1, 0, 0, 0, 11, 7, 5, 4, 9, 1, 1, 1, 0, 0, 0, 0)
DEPTH = (0, 3, 4, 3, 1, 2, 3, 2, 2, 3, 4, 3, 3, 4, 5, 4)
DEEPEST = max(DEPTH)
BLOCKS = 8
STEPS = BLOCKS + 4 + DEEPEST


def split(value):
    high = value.astype(BF16)
    return high, (value - high.astype(F32)).astype(BF16)


def mm(left, right):
    return jnp.dot(left, right, preferred_element_type=F32)


def dot3(left, right):
    lh, ll = split(left)
    rh, rl = split(right)
    return mm(lh, rh) + (mm(lh, rl) + mm(ll, rh))


def lookup(table, index):
    found = jnp.int32(table[0])
    for at in range(1, len(table)):
        found = jnp.where(index == at, jnp.int32(table[at]), found)
    return found


def kernel(
    g_hbm, l1_hbm, l2_hbm, h1_hbm, h2_hbm, w1_ref, w2_ref,
    a1_hbm, a2_hbm, d1_hbm, d2_hbm,
    gbuf, ghi, glo, lbuf, lthi, ltlo, hbuf, kbuf, zbuf, pbuf, xbuf, cbuf, sbuf, obuf,
    dacc2, dacc1, rs2, rs1, dfull, xfull,
    gsem, lsem, hsem, ksend, krecv, xsend, xrecv, csend, crecv, tsend, trecv, osem,
    rsend, rrecv, bsend, drecv, vsend, xxsend, xxrecv,
):
    p = lax.axis_index("prow")
    q = lax.axis_index("pcol")
    z, c = p // 2, p % 2
    y, x = q // 4, q % 4
    zd, cd = (q % 8) // 2, q % 2
    k = (z - zd + 4) % 4
    off_chip = k != 0
    is_dest = q % 8 == p
    helper = jnp.logical_and(k == 0, c != cd)
    pos = jnp.where(c == 0, k - 1, 3 - k)
    home = 2 * zd + cd
    is_root = jnp.logical_and(p == 0, q == 0)

    def remote(src, dst, send, recv, pp, qq):
        return pltpu.make_async_remote_copy(
            src_ref=src, dst_ref=dst, send_sem=send, recv_sem=recv,
            device_id={"prow": pp, "pcol": qq}, device_id_type=pl.DeviceIdType.MESH,
        )

    def load_l(panel):
        src = (l2_hbm, l1_hbm)[panel]
        return pltpu.make_async_copy(src.at[:, 0], lbuf.at[panel], lsem.at[panel])

    def load_g(col):
        return pltpu.make_async_copy(g_hbm.at[:, 0, :, col, 0, :], gbuf.at[col], gsem.at[col])

    def load_h(panel, col):
        src = (h2_hbm, h1_hbm)[panel]
        return pltpu.make_async_copy(src.at[2 * col + q // 8, 0], hbuf.at[panel, col], hsem.at[panel, col])

    load_l(0).start()
    load_l(1).start()
    for i in range(4):
        load_g((i + 1) % 4).start()

    @pl.when(is_dest)
    def _():
        for panel in range(2):
            for i in range(4):
                load_h(panel, (i + 1) % 4).start()

    barrier = pltpu.get_barrier_semaphore()

    def greet(pp, qq):
        pl.semaphore_signal(
            barrier, inc=1, device_id={"prow": pp, "pcol": qq}, device_id_type=pl.DeviceIdType.MESH
        )

    def greet_column(i, _):
        greet((p + i) % 8, q)
        return 0

    def greet_plane(i, _):
        greet(p, (q + i) % 16)
        return 0

    def greet_dest(i, _):
        other = (q + i) % 16

        @pl.when(i != 8)
        def _():
            greet(other % 8, other)

        return 0

    lax.fori_loop(1, 8, greet_column, 0)
    lax.fori_loop(1, 16, greet_plane, 0)

    @pl.when(is_dest)
    def _():
        lax.fori_loop(1, 16, greet_dest, 0)

    for panel in range(2):
        load_l(panel).wait()

        def turn(kb, _, panel=panel):
            hi, lo = split(lbuf[panel, kb].T)
            at = pl.ds(pl.multiple_of(kb * B, B), B)
            lthi[panel * B:(panel + 1) * B, at] = hi
            ltlo[panel * B:(panel + 1) * B, at] = lo
            return 0

        lax.fori_loop(0, 8, turn, 0)

    @pl.when(is_dest)
    def _():
        pl.semaphore_wait(barrier, 36)

    @pl.when(jnp.logical_not(is_dest))
    def _():
        pl.semaphore_wait(barrier, 22)

    corner = remote(l1_hbm.at[0, 0], kbuf, ksend, krecv, home, q)
    corner_here = pltpu.make_async_copy(l1_hbm.at[0, 0], kbuf, krecv)

    @pl.when(jnp.logical_and(p == 0, jnp.logical_not(is_dest)))
    def _():
        corner.start()

    @pl.when(jnp.logical_and(p == 0, is_dest))
    def _():
        corner_here.start()

    def swap_whole(n):
        return remote(pbuf.at[n], xbuf.at[n], xsend.at[n], xrecv.at[n], 2 * z + cd, q)

    def swap_half(n):
        rows = pl.ds(pl.multiple_of((1 - c) * HALF, HALF), HALF)
        return remote(
            pbuf.at[n, rows], xbuf.at[n, pl.ds(0, HALF)], xsend.at[n], xrecv.at[n], 2 * z + 1 - c, q
        )

    def products(i):
        col = (i + 1) % 4
        load_g(col).wait()

        def halve(kb, _):
            hi, lo = split(gbuf[col, kb])
            at = pl.ds(pl.multiple_of(kb * B, B), B)
            ghi[at, :] = hi
            glo[at, :] = lo
            return 0

        lax.fori_loop(0, 8, halve, 0)

        def one(panel, _):
            rows = pl.ds(pl.multiple_of(panel * B, B), B)
            lh = lthi[rows, :]
            pbuf[4 * panel + i] = mm(lh, ghi[...]) + (mm(lh, glo[...]) + mm(ltlo[rows, :], ghi[...]))

            @pl.when(helper)
            def _():
                swap_whole(4 * panel + i).start()

            @pl.when(off_chip)
            def _():
                swap_half(4 * panel + i).start()

            return 0

        lax.fori_loop(0, 2, one, 0)

    def pass_on(n):
        last = pos == 2
        zn = jnp.where(c == 0, (z + 1) % 4, (z + 3) % 4)
        cn = jnp.where(last, cd, c)
        return remote(sbuf.at[n], cbuf.at[n, c], csend.at[n], crecv.at[n, c], 2 * zn + cn, q)

    def got_sum(n, half):
        return remote(cbuf.at[n, half], cbuf.at[n, half], csend.at[n], crecv.at[n, half], home, q)

    def chain(n):
        swap_half(n).wait_recv()
        rows = pl.ds(pl.multiple_of(c * HALF, HALF), HALF)
        sbuf[n] = pbuf[n, rows, :] + xbuf[n, 0:HALF, :]

        @pl.when(pos > 0)
        def _():
            got_sum(n, c).wait_recv()
            sbuf[n] += cbuf[n, c]

        pass_on(n).start()

    def whole_sum(n):
        swap_whole(n).wait_recv()
        got_sum(n, 0).wait_recv()
        got_sum(n, 1).wait_recv()
        xbuf[n] += pbuf[n]
        xbuf[n, 0:HALF, :] += cbuf[n, 0]
        xbuf[n, HALF:B, :] += cbuf[n, 1]
        return xbuf[n]

    def finish_two(n):
        col = (n + 1) % 4
        r = 2 * col + q // 8
        total = whole_sum(n)
        load_h(0, col).wait()
        resid = hbuf[0, col].T - 2.0 * total
        at = dot3(w2_ref[...].T, resid)
        obuf[0, r] = at.T
        dacc2[:, 0:16, :] += dot3(at, lbuf[0, r]).reshape(16, 16, B)
        dacc2[:, 16:32, :] += dot3(at, lbuf[1, r]).reshape(16, 16, B)
        zbuf[col] = SCALE * dot3(kbuf[...].T, at)

    def finish_one(n):
        col = (n + 1) % 4
        r = 2 * col + q // 8
        total = whole_sum(n)
        load_h(1, col).wait()
        resid = hbuf[1, col].T - 2.0 * total - zbuf[col]
        xbuf[n] = resid

        @pl.when(jnp.logical_and(is_root, n == 7))
        def _():
            def got(i, _):
                send_cross(i).wait_recv()
                return 0

            lax.fori_loop(1, 16, got, 0)
            xbuf[n] -= xfull[...].T

        at = dot3(w1_ref[...].T, xbuf[n])
        obuf[1, r] = at.T
        dacc1[...] += dot3(at, lbuf[1, r]).reshape(16, 16, B)

    def rows16(j):
        return pl.ds(pl.multiple_of(j * 16, 16), 16)

    def spread(rnd, j, me):
        src, dst = ((dacc2, rs2), (dacc1, rs1))[rnd]
        return remote(src.at[j], dst.at[me], rsend.at[rnd, j], rrecv.at[rnd, me], j % 8, j)

    def spread_all(rnd):
        def send(i, _):
            spread(rnd, (q + i) % 16, q).start()
            return 0

        lax.fori_loop(1, 16, send, 0)

    def send_cross(j):
        return remote(xfull.at[rows16(j)], xfull.at[rows16(j)], xxsend, xxrecv.at[j], 0, 0)

    def to_plane(rnd, i):
        mine = dfull.at[rnd, rows16(q)]
        return remote(mine, mine, bsend.at[rnd, i], drecv.at[rnd, q], p, (q + i) % 16)

    def own_rows(rnd):
        src, dst = ((dacc2, rs2), (dacc1, rs1))[rnd]

        def add(i, acc):
            j = (q + i) % 16
            spread(rnd, q, j).wait_recv()
            return acc + dst[j]

        total = lax.fori_loop(1, 16, add, src[q])
        dfull[rnd, rows16(q), :] = -SCALE * total[0:16]
        if rnd == 0:
            xfull[rows16(q), :] = SCALE * total[16:32]

            @pl.when(jnp.logical_not(is_root))
            def _():
                send_cross(q).start()

        def send(i, _):
            to_plane(rnd, i).start()
            return 0

        lax.fori_loop(1, 16, send, 0)

    def slice_copy(rnd, j, i):
        here = dfull.at[rnd, rows16(j)]
        return remote(here, here, vsend.at[rnd, j // 8, i], drecv.at[rnd, j], (p + i) % 8, q)

    def to_column(rnd):
        for h in range(2):
            j = p + 8 * h

            @pl.when(j != q)
            def _(j=j):
                slice_copy(rnd, j, 0).wait_recv()

            def send(i, _, j=j):
                slice_copy(rnd, j, i).start()
                return 0

            lax.fori_loop(1, 8, send, 0)

    flows = []
    for h in range(2):
        qs = p + 8 * h
        dx = (x - qs % 4 + 4) % 4
        dy = (y - qs // 4 + 4) % 4
        for turn_by in range(4):
            u, v = ((dx, dy), (dy, (4 - dx) % 4), ((4 - dx) % 4, (4 - dy) % 4), ((4 - dy) % 4, dx))[turn_by]
            flows.append((h, turn_by, lookup(CHILDREN, 4 * u + v), lookup(DEPTH, 4 * u + v)))
    sides = (4 * y + (x + 1) % 4, 4 * ((y + 1) % 4) + x, 4 * y + (x + 3) % 4, 4 * ((y + 3) % 4) + x)

    def tile_part(n, f):
        h, turn_by, _, _ = flows[f]
        return obuf.at[n // 4, 2 * ((n + 1) % 4) + h, pl.ds(QUARTER * turn_by, QUARTER), :]

    def branch(n, f, e):
        part = tile_part(n, f)
        return remote(
            part, part, tsend.at[n % 2, f, e], trecv.at[n, f], p, sides[(e + flows[f][1]) % 4]
        )

    def has_branch(f, e):
        return (flows[f][2] // (1 << e)) % 2 == 1

    def store(n, f):
        h, turn_by, _, _ = flows[f]
        r = 2 * ((n + 1) % 4) + h
        rows = pl.ds(QUARTER * turn_by, QUARTER)

        @pl.when(n < 4)
        def _():
            pltpu.make_async_copy(tile_part(n, f), a2_hbm.at[r, 0, rows, :], osem.at[0]).start()

        @pl.when(n >= 4)
        def _():
            pltpu.make_async_copy(tile_part(n, f), a1_hbm.at[r, 0, rows, :], osem.at[1]).start()

    def forward(t, f):
        depth = flows[f][3]
        n = t - 4 - depth

        @pl.when(jnp.logical_and(n >= 0, n < BLOCKS))
        def _():
            @pl.when(depth > 0)
            def _():
                branch(n, f, 0).wait_recv()

            for e in range(4):
                @pl.when(has_branch(f, e))
                def _(e=e):
                    @pl.when(n >= 2)
                    def _():
                        branch(n - 2, f, e).wait_send()

                    branch(n, f, e).start()

            store(n, f)

    def step(t, _):
        @pl.when(t < 4)
        def _():
            products(t)

        ahead = t - 1 - pos

        @pl.when(jnp.logical_and(off_chip, jnp.logical_and(ahead >= 0, ahead < BLOCKS)))
        def _():
            chain(ahead)

        @pl.when(is_dest)
        def _():
            @pl.when(t == 4)
            def _():
                dacc2[...] = jnp.zeros_like(dacc2)
                dacc1[...] = jnp.zeros_like(dacc1)
                corner_here.wait()

            @pl.when(t == 8)
            def _():
                own_rows(0)

            @pl.when(t == 12)
            def _():
                own_rows(1)

            @pl.when(jnp.logical_and(t >= 4, t < 8))
            def _():
                finish_two(t - 4)

            @pl.when(t == 7)
            def _():
                spread_all(0)

            @pl.when(jnp.logical_and(t >= 8, t < 12))
            def _():
                finish_one(t - 4)

            @pl.when(t == 11)
            def _():
                spread_all(1)

        @pl.when(t == 10)
        def _():
            to_column(0)

        @pl.when(t == 13)
        def _():
            to_column(1)

        for f in range(8):
            forward(t, f)
        return 0

    lax.fori_loop(0, STEPS, step, 0)

    for rnd, out in ((0, d2_hbm), (1, d1_hbm)):
        for h in range(2):
            def late(i, _, rnd=rnd, h=h):
                slice_copy(rnd, (p + i) % 8 + 8 * h, 0).wait_recv()
                return 0

            lax.fori_loop(1, 8, late, 0)
        pltpu.make_async_copy(dfull.at[rnd], out, osem.at[2 + rnd]).start()

    def sent(n, _):
        @pl.when(helper)
        def _():
            swap_whole(n).wait_send()

        @pl.when(off_chip)
        def _():
            swap_half(n).wait_send()
            pass_on(n).wait_send()

        return 0

    lax.fori_loop(0, BLOCKS, sent, 0)

    @pl.when(jnp.logical_and(p == 0, jnp.logical_not(is_dest)))
    def _():
        corner.wait_send()

    for f in range(8):
        for e in range(4):
            @pl.when(has_branch(f, e))
            def _(f=f, e=e):
                branch(6, f, e).wait_send()
                branch(7, f, e).wait_send()

    for rnd in range(2):
        for h in range(2):
            def column_sent(i, _, rnd=rnd, h=h):
                slice_copy(rnd, p + 8 * h, i).wait_send()
                return 0

            lax.fori_loop(1, 8, column_sent, 0)

        @pl.when(is_dest)
        def _(rnd=rnd):
            def home_sent(i, _):
                spread(rnd, (q + i) % 16, q).wait_send()
                to_plane(rnd, i).wait_send()
                return 0

            lax.fori_loop(1, 16, home_sent, 0)

    @pl.when(jnp.logical_and(is_dest, jnp.logical_not(is_root)))
    def _():
        send_cross(q).wait_send()

    pltpu.make_async_copy(obuf.at[0], a2_hbm.at[:, 0], osem.at[0]).wait()
    pltpu.make_async_copy(obuf.at[1], a1_hbm.at[:, 0], osem.at[1]).wait()
    pltpu.make_async_copy(dfull.at[0], d2_hbm, osem.at[2]).wait()
    pltpu.make_async_copy(dfull.at[1], d1_hbm, osem.at[3]).wait()


def local(grad_trailing, panel_one, panel_two, grad_one, grad_two, inv_one, inv_two):
    any_space = pl.BlockSpec(memory_space=pl.ANY)
    vmem = pl.BlockSpec(memory_space=pltpu.VMEM)
    panel = jax.ShapeDtypeStruct(panel_one.shape, F32)
    square = jax.ShapeDtypeStruct((B, B), F32)
    dma = pltpu.SemaphoreType.DMA
    return pl.pallas_call(
        kernel,
        out_shape=(panel, panel, square, square),
        in_specs=[any_space] * 5 + [vmem] * 2,
        out_specs=(any_space,) * 4,
        scratch_shapes=[
            pltpu.VMEM((4, 8, B, B), F32),
            pltpu.VMEM((8 * B, B), BF16),
            pltpu.VMEM((8 * B, B), BF16),
            pltpu.VMEM((2, 8, B, B), F32),
            pltpu.VMEM((2 * B, 8 * B), BF16),
            pltpu.VMEM((2 * B, 8 * B), BF16),
            pltpu.VMEM((2, 4, B, B), F32),
            pltpu.VMEM((B, B), F32),
            pltpu.VMEM((4, B, B), F32),
            pltpu.VMEM((BLOCKS, B, B), F32),
            pltpu.VMEM((BLOCKS, B, B), F32),
            pltpu.VMEM((BLOCKS, 2, HALF, B), F32),
            pltpu.VMEM((BLOCKS, HALF, B), F32),
            pltpu.VMEM((2, 8, B, B), F32),
            pltpu.VMEM((16, 32, B), F32),
            pltpu.VMEM((16, 16, B), F32),
            pltpu.VMEM((16, 32, B), F32),
            pltpu.VMEM((16, 16, B), F32),
            pltpu.VMEM((2, B, B), F32),
            pltpu.VMEM((B, B), F32),
            dma((4,)),
            dma((2,)),
            dma((2, 4)),
            dma,
            dma,
            dma((BLOCKS,)),
            dma((BLOCKS,)),
            dma((BLOCKS,)),
            dma((BLOCKS, 2)),
            dma((2, 8, 4)),
            dma((BLOCKS, 8)),
            dma((4,)),
            dma((2, 16)),
            dma((2, 16)),
            dma((2, 16)),
            dma((2, 16)),
            dma((2, 2, 8)),
            dma,
            dma((16,)),
        ],
        compiler_params=pltpu.CompilerParams(
            collective_id=0, has_side_effects=True, vmem_limit_bytes=56 * 2**20
        ),
        cost_estimate=pl.CostEstimate(flops=7_000_000_000, bytes_accessed=22_000_000, transcendentals=0),
    )(grad_trailing, panel_one, panel_two, grad_one, grad_two, inv_one, inv_two)


def solution(mesh):
    placed = (
        P(None, "prow", None, None, "pcol", None),
        P(None, "prow", None, None),
        P(None, "prow", None, None),
        P(None, "prow", None, None),
        P(None, "prow", None, None),
        P(),
        P(),
    )
    return jax.shard_map(
        local,
        mesh=mesh,
        in_specs=placed,
        out_specs=(P(None, "prow", None, None), P(None, "prow", None, None), P(), P()),
        check_vma=False,
    )
```

```python
import math

import jax
import jax.numpy as jnp
from jax import lax
from jax.experimental import pallas as pl
from jax.experimental.pallas import tpu as pltpu
from jax.sharding import PartitionSpec as P

N = 16384
B = 256
HALF = B // 2
QUARTER = B // 4
SCALE = 1.0 / math.sqrt(N)
F32 = jnp.float32
BF16 = jnp.bfloat16

CHILDREN = (1, 0, 0, 0, 11, 7, 5, 4, 9, 1, 1, 1, 0, 0, 0, 0)
DEPTH = (0, 3, 4, 3, 1, 2, 3, 2, 2, 3, 4, 3, 3, 4, 5, 4)
DEEPEST = max(DEPTH)
BLOCKS = 8
HOP = 4
START = 1 + 3 * HOP
TREE = 2
STEPS = START + BLOCKS + TREE * DEEPEST
FINISHED = (1, 2, 4, 6, 7, 7, 8)


def split(value):
    high = value.astype(BF16)
    return high, (value - high.astype(F32)).astype(BF16)


def mm(left, right):
    return jnp.dot(left, right, preferred_element_type=F32)


def dot3(left, right):
    lh, ll = split(left)
    rh, rl = split(right)
    return mm(lh, rh) + (mm(lh, rl) + mm(ll, rh))


def lookup(table, index):
    found = jnp.int32(table[0])
    for at in range(1, len(table)):
        found = jnp.where(index == at, jnp.int32(table[at]), found)
    return found


def kernel(
    g_hbm, l1_hbm, l2_hbm, h1_hbm, h2_hbm, w1_ref, w2_ref,
    a1_hbm, a2_hbm, d1_hbm, d2_hbm,
    gbuf, ghi, glo, turned_hi, turned_lo, lbuf, lthi, ltlo, hbuf, kbuf, zbuf, pbuf, xbuf, cbuf, sbuf, obuf,
    dacc2, dacc1, rs2, rs1, dfull, xfull,
    gsem, lsem, hsem, ksend, krecv, xsend, xrecv, csend, crecv, tsend, trecv, osem,
    rsend, rrecv, bsend, drecv, vsend, xxsend, xxrecv,
):
    p = lax.axis_index("prow")
    q = lax.axis_index("pcol")
    z, c = p // 2, p % 2
    y, x = q // 4, q % 4
    zd, cd = (q % 8) // 2, q % 2
    k = (z - zd + 4) % 4
    off_chip = k != 0
    is_dest = q % 8 == p
    helper = jnp.logical_and(k == 0, c != cd)
    pos = jnp.where(c == 0, k - 1, 3 - k)
    home = 2 * zd + cd
    is_root = jnp.logical_and(p == 0, q == 0)

    def remote(src, dst, send, recv, pp, qq):
        return pltpu.make_async_remote_copy(
            src_ref=src, dst_ref=dst, send_sem=send, recv_sem=recv,
            device_id={"prow": pp, "pcol": qq}, device_id_type=pl.DeviceIdType.MESH,
        )

    def load_l(panel):
        src = (l2_hbm, l1_hbm)[panel]
        return pltpu.make_async_copy(src.at[:, 0], lbuf.at[panel], lsem.at[panel])

    def load_g(col):
        return pltpu.make_async_copy(g_hbm.at[:, 0, :, col, 0, :], gbuf.at[col], gsem.at[col])

    def load_h(panel, col):
        src = (h2_hbm, h1_hbm)[panel]
        return pltpu.make_async_copy(src.at[2 * col + q // 8, 0], hbuf.at[panel, col], hsem.at[panel, col])

    load_l(0).start()
    load_l(1).start()
    for i in range(4):
        load_g((i + 1) % 4).start()

    @pl.when(is_dest)
    def _():
        for panel in range(2):
            for i in range(4):
                load_h(panel, (i + 1) % 4).start()

    barrier = pltpu.get_barrier_semaphore()

    def greet(pp, qq):
        pl.semaphore_signal(
            barrier, inc=1, device_id={"prow": pp, "pcol": qq}, device_id_type=pl.DeviceIdType.MESH
        )

    def greet_column(i, _):
        greet((p + i) % 8, q)
        return 0

    def greet_plane(i, _):
        greet(p, (q + i) % 16)
        return 0

    def greet_dest(i, _):
        other = (q + i) % 16

        @pl.when(i != 8)
        def _():
            greet(other % 8, other)

        return 0

    lax.fori_loop(1, 8, greet_column, 0)
    lax.fori_loop(1, 16, greet_plane, 0)

    @pl.when(is_dest)
    def _():
        lax.fori_loop(1, 16, greet_dest, 0)

    for panel in range(2):
        load_l(panel).wait()

        def turn(kb, _, panel=panel):
            hi, lo = split(lbuf[panel, kb].T)
            at = pl.ds(pl.multiple_of(kb * B, B), B)
            lthi[panel * B:(panel + 1) * B, at] = hi
            ltlo[panel * B:(panel + 1) * B, at] = lo
            return 0

        lax.fori_loop(0, 8, turn, 0)

    @pl.when(is_dest)
    def _():
        pl.semaphore_wait(barrier, 36)

    @pl.when(jnp.logical_not(is_dest))
    def _():
        pl.semaphore_wait(barrier, 22)

    corner = remote(l1_hbm.at[0, 0], kbuf, ksend, krecv, home, q)
    corner_here = pltpu.make_async_copy(l1_hbm.at[0, 0], kbuf, krecv)

    @pl.when(jnp.logical_and(p == 0, jnp.logical_not(is_dest)))
    def _():
        corner.start()

    @pl.when(jnp.logical_and(p == 0, is_dest))
    def _():
        corner_here.start()

    def swap_whole(n):
        return remote(pbuf.at[n], xbuf.at[n], xsend.at[n], xrecv.at[n], 2 * z + cd, q)

    def swap_half(n):
        rows = pl.ds(pl.multiple_of((1 - c) * HALF, HALF), HALF)
        return remote(
            pbuf.at[n, rows], xbuf.at[n, pl.ds(0, HALF)], xsend.at[n], xrecv.at[n], 2 * z + 1 - c, q
        )

    def products(n):
        col = (n + 1) % 4
        panel = n // 4

        @pl.when(n < 4)
        def _():
            load_g(col).wait()

            def halve(kb, _):
                hi, lo = split(gbuf[col, kb])
                at = pl.ds(pl.multiple_of(kb * B, B), B)
                ghi[col, at, :] = hi
                glo[col, at, :] = lo
                return 0

            lax.fori_loop(0, 8, halve, 0)

        rows = pl.ds(pl.multiple_of(panel * B, B), B)
        lh = lthi[rows, :]
        pbuf[n] = mm(lh, ghi[col]) + (mm(lh, glo[col]) + mm(ltlo[rows, :], ghi[col]))

        @pl.when(helper)
        def _():
            swap_whole(n).start()

        @pl.when(off_chip)
        def _():
            swap_half(n).start()

    def pass_on(n):
        last = pos == 2
        zn = jnp.where(c == 0, (z + 1) % 4, (z + 3) % 4)
        cn = jnp.where(last, cd, c)
        return remote(sbuf.at[n], cbuf.at[n, c], csend.at[n], crecv.at[n, c], 2 * zn + cn, q)

    def got_sum(n, half):
        return remote(cbuf.at[n, half], cbuf.at[n, half], csend.at[n], crecv.at[n, half], home, q)

    def chain(n):
        swap_half(n).wait_recv()
        rows = pl.ds(pl.multiple_of(c * HALF, HALF), HALF)
        sbuf[n] = pbuf[n, rows, :] + xbuf[n, 0:HALF, :]

        @pl.when(pos > 0)
        def _():
            got_sum(n, c).wait_recv()
            sbuf[n] += cbuf[n, c]

        pass_on(n).start()

    def whole_sum(n):
        swap_whole(n).wait_recv()
        got_sum(n, 0).wait_recv()
        got_sum(n, 1).wait_recv()
        xbuf[n] += pbuf[n]
        xbuf[n, 0:HALF, :] += cbuf[n, 0]
        xbuf[n, HALF:B, :] += cbuf[n, 1]
        return xbuf[n]

    def keep_turned(i, value):
        hi, lo = split(value.T)
        turned_hi[i] = hi
        turned_lo[i] = lo

    def turned_dot3(i, right):
        rh, rl = split(right)
        lh = turned_hi[i]
        return mm(lh, rh) + (mm(lh, rl) + mm(turned_lo[i], rh))

    def finish_two(n):
        col = (n + 1) % 4
        r = 2 * col + q // 8
        total = whole_sum(n)
        load_h(0, col).wait()
        resid = hbuf[0, col].T - 2.0 * total
        at = turned_dot3(0, resid)
        obuf[0, r] = at.T
        dacc2[:, 0:16, :] += dot3(at, lbuf[0, r]).reshape(16, 16, B)
        dacc2[:, 16:32, :] += dot3(at, lbuf[1, r]).reshape(16, 16, B)
        zbuf[col] = SCALE * turned_dot3(2, at)

    def finish_one(n):
        col = (n + 1) % 4
        r = 2 * col + q // 8
        total = whole_sum(n)
        load_h(1, col).wait()
        resid = hbuf[1, col].T - 2.0 * total - zbuf[col]
        xbuf[n] = resid

        @pl.when(jnp.logical_and(is_root, n == 7))
        def _():
            def got(i, _):
                send_cross(i).wait_recv()
                return 0

            lax.fori_loop(1, 16, got, 0)
            xbuf[n] -= xfull[...].T

        at = turned_dot3(1, xbuf[n])
        obuf[1, r] = at.T
        dacc1[...] += dot3(at, lbuf[1, r]).reshape(16, 16, B)

    def rows16(j):
        return pl.ds(pl.multiple_of(j * 16, 16), 16)

    def spread(rnd, j, me):
        src, dst = ((dacc2, rs2), (dacc1, rs1))[rnd]
        return remote(src.at[j], dst.at[me], rsend.at[rnd, j], rrecv.at[rnd, me], j % 8, j)

    def spread_all(rnd):
        def send(i, _):
            spread(rnd, (q + i) % 16, q).start()
            return 0

        lax.fori_loop(1, 16, send, 0)

    def send_cross(j):
        return remote(xfull.at[rows16(j)], xfull.at[rows16(j)], xxsend, xxrecv.at[j], 0, 0)

    def to_plane(rnd, i):
        mine = dfull.at[rnd, rows16(q)]
        return remote(mine, mine, bsend.at[rnd, i], drecv.at[rnd, q], p, (q + i) % 16)

    def own_rows(rnd):
        src, dst = ((dacc2, rs2), (dacc1, rs1))[rnd]

        def add(i, acc):
            j = (q + i) % 16
            spread(rnd, q, j).wait_recv()
            return acc + dst[j]

        total = lax.fori_loop(1, 16, add, src[q])
        dfull[rnd, rows16(q), :] = -SCALE * total[0:16]
        if rnd == 0:
            xfull[rows16(q), :] = SCALE * total[16:32]

            @pl.when(jnp.logical_not(is_root))
            def _():
                send_cross(q).start()

        def send(i, _):
            to_plane(rnd, i).start()
            return 0

        lax.fori_loop(1, 16, send, 0)

    def slice_copy(rnd, j, i):
        here = dfull.at[rnd, rows16(j)]
        return remote(here, here, vsend.at[rnd, j // 8, i], drecv.at[rnd, j], (p + i) % 8, q)

    def to_column(rnd):
        for h in range(2):
            j = p + 8 * h

            @pl.when(j != q)
            def _(j=j):
                slice_copy(rnd, j, 0).wait_recv()

            def send(i, _, j=j):
                slice_copy(rnd, j, i).start()
                return 0

            lax.fori_loop(1, 8, send, 0)

    flows = []
    for h in range(2):
        qs = p + 8 * h
        dx = (x - qs % 4 + 4) % 4
        dy = (y - qs // 4 + 4) % 4
        for turn_by in range(4):
            u, v = ((dx, dy), (dy, (4 - dx) % 4), ((4 - dx) % 4, (4 - dy) % 4), ((4 - dy) % 4, dx))[turn_by]
            flows.append((h, turn_by, lookup(CHILDREN, 4 * u + v), lookup(DEPTH, 4 * u + v)))
    sides = (4 * y + (x + 1) % 4, 4 * ((y + 1) % 4) + x, 4 * y + (x + 3) % 4, 4 * ((y + 3) % 4) + x)

    def tile_part(n, f):
        h, turn_by, _, _ = flows[f]
        return obuf.at[n // 4, 2 * ((n + 1) % 4) + h, pl.ds(QUARTER * turn_by, QUARTER), :]

    def branch(n, f, e):
        part = tile_part(n, f)
        return remote(
            part, part, tsend.at[n % 2, f, e], trecv.at[n, f], p, sides[(e + flows[f][1]) % 4]
        )

    def has_branch(f, e):
        return (flows[f][2] // (1 << e)) % 2 == 1

    def store(n, f):
        h, turn_by, _, _ = flows[f]
        r = 2 * ((n + 1) % 4) + h
        rows = pl.ds(QUARTER * turn_by, QUARTER)

        @pl.when(n < 4)
        def _():
            pltpu.make_async_copy(tile_part(n, f), a2_hbm.at[r, 0, rows, :], osem.at[0]).start()

        @pl.when(n >= 4)
        def _():
            pltpu.make_async_copy(tile_part(n, f), a1_hbm.at[r, 0, rows, :], osem.at[1]).start()

    def forward(t, f):
        depth = flows[f][3]
        n = t - START - TREE * depth

        @pl.when(jnp.logical_and(n >= 0, n < BLOCKS))
        def _():
            @pl.when(depth > 0)
            def _():
                branch(n, f, 0).wait_recv()

            for e in range(4):
                @pl.when(has_branch(f, e))
                def _(e=e):
                    @pl.when(n >= 2)
                    def _():
                        branch(n - 2, f, e).wait_send()

                    branch(n, f, e).start()

            store(n, f)

    def step(t, _):
        @pl.when(t < BLOCKS)
        def _():
            products(t)

        ahead = t - 1 - HOP * pos

        @pl.when(jnp.logical_and(off_chip, jnp.logical_and(ahead >= 0, ahead < BLOCKS)))
        def _():
            chain(ahead)

        since = t - START

        @pl.when(is_dest)
        def _():
            @pl.when(since == -1)
            def _():
                dacc2[...] = jnp.zeros_like(dacc2)
                dacc1[...] = jnp.zeros_like(dacc1)
                keep_turned(0, w2_ref[...])
                keep_turned(1, w1_ref[...])
                corner_here.wait()
                keep_turned(2, kbuf[...])

            @pl.when(since == 4)
            def _():
                own_rows(0)

            @pl.when(since == 8)
            def _():
                own_rows(1)

            def finish(n, _):
                @pl.when(n < 4)
                def _():
                    finish_two(n)

                @pl.when(n >= 4)
                def _():
                    finish_one(n)

                return 0

            done = jnp.where(since < len(FINISHED), lookup(FINISHED, since), BLOCKS)
            before = lookup((0,) + FINISHED, since)

            @pl.when(jnp.logical_and(since >= 0, since < len(FINISHED)))
            def _():
                lax.fori_loop(before, done, finish, 0)

            @pl.when(since == 2)
            def _():
                spread_all(0)

            @pl.when(since == 6)
            def _():
                spread_all(1)

        @pl.when(since == 7)
        def _():
            to_column(0)

        @pl.when(since == 11)
        def _():
            to_column(1)

        for f in range(8):
            forward(t, f)
        return 0

    lax.fori_loop(0, STEPS, step, 0)

    for rnd, out in ((0, d2_hbm), (1, d1_hbm)):
        for h in range(2):
            def late(i, _, rnd=rnd, h=h):
                slice_copy(rnd, (p + i) % 8 + 8 * h, 0).wait_recv()
                return 0

            lax.fori_loop(1, 8, late, 0)
        pltpu.make_async_copy(dfull.at[rnd], out, osem.at[2 + rnd]).start()

    def sent(n, _):
        @pl.when(helper)
        def _():
            swap_whole(n).wait_send()

        @pl.when(off_chip)
        def _():
            swap_half(n).wait_send()
            pass_on(n).wait_send()

        return 0

    lax.fori_loop(0, BLOCKS, sent, 0)

    @pl.when(jnp.logical_and(p == 0, jnp.logical_not(is_dest)))
    def _():
        corner.wait_send()

    for f in range(8):
        for e in range(4):
            @pl.when(has_branch(f, e))
            def _(f=f, e=e):
                branch(6, f, e).wait_send()
                branch(7, f, e).wait_send()

    for rnd in range(2):
        for h in range(2):
            def column_sent(i, _, rnd=rnd, h=h):
                slice_copy(rnd, p + 8 * h, i).wait_send()
                return 0

            lax.fori_loop(1, 8, column_sent, 0)

        @pl.when(is_dest)
        def _(rnd=rnd):
            def home_sent(i, _):
                spread(rnd, (q + i) % 16, q).wait_send()
                to_plane(rnd, i).wait_send()
                return 0

            lax.fori_loop(1, 16, home_sent, 0)

    @pl.when(jnp.logical_and(is_dest, jnp.logical_not(is_root)))
    def _():
        send_cross(q).wait_send()

    pltpu.make_async_copy(obuf.at[0], a2_hbm.at[:, 0], osem.at[0]).wait()
    pltpu.make_async_copy(obuf.at[1], a1_hbm.at[:, 0], osem.at[1]).wait()
    pltpu.make_async_copy(dfull.at[0], d2_hbm, osem.at[2]).wait()
    pltpu.make_async_copy(dfull.at[1], d1_hbm, osem.at[3]).wait()


def hand_over(*refs):
    sems = refs[8]
    copies = [pltpu.make_async_copy(refs[i], refs[4 + i], sems.at[i]) for i in range(4)]
    for copy in copies:
        copy.start()
    for copy in copies:
        copy.wait()


def local(grad_trailing, panel_one, panel_two, grad_one, grad_two, inv_one, inv_two):
    any_space = pl.BlockSpec(memory_space=pl.ANY)
    vmem = pl.BlockSpec(memory_space=pltpu.VMEM)
    panel = jax.ShapeDtypeStruct(panel_one.shape, F32)
    square = jax.ShapeDtypeStruct((B, B), F32)
    dma = pltpu.SemaphoreType.DMA
    results = pl.pallas_call(
        kernel,
        out_shape=(panel, panel, square, square),
        in_specs=[any_space] * 5 + [vmem] * 2,
        out_specs=(any_space,) * 4,
        scratch_shapes=[
            pltpu.VMEM((4, 8, B, B), F32),
            pltpu.VMEM((4, 8 * B, B), BF16),
            pltpu.VMEM((4, 8 * B, B), BF16),
            pltpu.VMEM((3, B, B), BF16),
            pltpu.VMEM((3, B, B), BF16),
            pltpu.VMEM((2, 8, B, B), F32),
            pltpu.VMEM((2 * B, 8 * B), BF16),
            pltpu.VMEM((2 * B, 8 * B), BF16),
            pltpu.VMEM((2, 4, B, B), F32),
            pltpu.VMEM((B, B), F32),
            pltpu.VMEM((4, B, B), F32),
            pltpu.VMEM((BLOCKS, B, B), F32),
            pltpu.VMEM((BLOCKS, B, B), F32),
            pltpu.VMEM((BLOCKS, 2, HALF, B), F32),
            pltpu.VMEM((BLOCKS, HALF, B), F32),
            pltpu.VMEM((2, 8, B, B), F32),
            pltpu.VMEM((16, 32, B), F32),
            pltpu.VMEM((16, 16, B), F32),
            pltpu.VMEM((16, 32, B), F32),
            pltpu.VMEM((16, 16, B), F32),
            pltpu.VMEM((2, B, B), F32),
            pltpu.VMEM((B, B), F32),
            dma((4,)),
            dma((2,)),
            dma((2, 4)),
            dma,
            dma,
            dma((BLOCKS,)),
            dma((BLOCKS,)),
            dma((BLOCKS,)),
            dma((BLOCKS, 2)),
            dma((2, 8, 4)),
            dma((BLOCKS, 8)),
            dma((4,)),
            dma((2, 16)),
            dma((2, 16)),
            dma((2, 16)),
            dma((2, 16)),
            dma((2, 2, 8)),
            dma,
            dma((16,)),
        ],
        compiler_params=pltpu.CompilerParams(
            collective_id=0, has_side_effects=True, vmem_limit_bytes=56 * 2**20
        ),
        cost_estimate=pl.CostEstimate(flops=7_000_000_000, bytes_accessed=22_000_000, transcendentals=0),
    )(grad_trailing, panel_one, panel_two, grad_one, grad_two, inv_one, inv_two)
    return pl.pallas_call(
        hand_over,
        out_shape=(panel, panel, square, square),
        in_specs=[any_space] * 4,
        out_specs=(any_space,) * 4,
        scratch_shapes=[dma((4,))],
    )(*results)


def solution(mesh):
    placed = (
        P(None, "prow", None, None, "pcol", None),
        P(None, "prow", None, None),
        P(None, "prow", None, None),
        P(None, "prow", None, None),
        P(None, "prow", None, None),
        P(),
        P(),
    )
    return jax.shard_map(
        local,
        mesh=mesh,
        in_specs=placed,
        out_specs=(P(None, "prow", None, None), P(None, "prow", None, None), P(), P()),
        check_vma=False,
    )
```

```python
import math

import jax
import jax.numpy as jnp
from jax import lax
from jax.experimental import pallas as pl
from jax.experimental.pallas import tpu as pltpu
from jax.sharding import PartitionSpec as P

N = 16384
B = 256
HALF = B // 2
QUARTER = B // 4
SCALE = 1.0 / math.sqrt(N)
F32 = jnp.float32
BF16 = jnp.bfloat16

CHILDREN = (1, 0, 0, 0, 11, 7, 5, 4, 9, 1, 1, 1, 0, 0, 0, 0)
DEPTH = (0, 3, 4, 3, 1, 2, 3, 2, 2, 3, 4, 3, 3, 4, 5, 4)
DEEPEST = max(DEPTH)
BLOCKS = 8
HOP = 3
START = 1 + 3 * HOP
TREE = 2
FINISHED = (1, 3, 4, 6, 7, 7, 7, 8)
SPREAD = (2, 7)
OWN = (5, 10)
COLUMN = (8, 13)
LAST = BLOCKS - 1 + TREE * DEEPEST
NEVER = 1 << 20


def split(value):
    high = value.astype(BF16)
    return high, (value - high.astype(F32)).astype(BF16)


def mm(left, right):
    return jnp.dot(left, right, preferred_element_type=F32)


def dot3(left, right):
    lh, ll = split(left)
    rh, rl = split(right)
    return mm(lh, rh) + (mm(lh, rl) + mm(ll, rh))


def lookup(table, index):
    found = jnp.int32(table[0])
    for at in range(1, len(table)):
        found = jnp.where(index == at, jnp.int32(table[at]), found)
    return found


def kernel(
    g_hbm, l1_hbm, l2_hbm, h1_hbm, h2_hbm, w1_ref, w2_ref,
    a1_hbm, a2_hbm, d1_hbm, d2_hbm,
    gbuf, ghi, glo, turned_hi, turned_lo, lbuf, lthi, ltlo, hbuf, kbuf, zbuf, pbuf, xbuf, cbuf, sbuf, obuf, atbuf,
    dacc2, dacc1, rs2, rs1, dfull, xfull,
    gsem, lsem, hsem, ksend, krecv, xsend, xrecv, csend, crecv, tsend, trecv, osem,
    rsend, rrecv, bsend, brecv, drecv, vsend, xxsend, xxrecv,
):
    p = lax.axis_index("prow")
    q = lax.axis_index("pcol")
    z, c = p // 2, p % 2
    y, x = q // 4, q % 4
    zd, cd = (q % 8) // 2, q % 2
    k = (z - zd + 4) % 4
    off_chip = k != 0
    is_dest = q % 8 == p
    helper = jnp.logical_and(k == 0, c != cd)
    pos = jnp.where(c == 0, k - 1, 3 - k)
    home = 2 * zd + cd
    is_root = jnp.logical_and(p == 0, q == 0)

    def remote(src, dst, send, recv, pp, qq):
        return pltpu.make_async_remote_copy(
            src_ref=src, dst_ref=dst, send_sem=send, recv_sem=recv,
            device_id={"prow": pp, "pcol": qq}, device_id_type=pl.DeviceIdType.MESH,
        )

    def load_l(panel):
        src = (l2_hbm, l1_hbm)[panel]
        return pltpu.make_async_copy(src.at[:, 0], lbuf.at[panel], lsem.at[panel])

    def load_g(col):
        return pltpu.make_async_copy(g_hbm.at[:, 0, :, col, 0, :], gbuf.at[col], gsem.at[col])

    def load_h(panel, col):
        src = (h2_hbm, h1_hbm)[panel]
        return pltpu.make_async_copy(src.at[2 * col + q // 8, 0], hbuf.at[panel, col], hsem.at[panel, col])

    load_l(0).start()
    load_l(1).start()
    for i in range(4):
        load_g((i + 1) % 4).start()

    @pl.when(is_dest)
    def _():
        for panel in range(2):
            for i in range(4):
                load_h(panel, (i + 1) % 4).start()

    flows = []
    for h in range(2):
        qs = p + 8 * h
        dx = (x - qs % 4 + 4) % 4
        dy = (y - qs // 4 + 4) % 4
        for turn_by in range(4):
            u, v = ((dx, dy), (dy, (4 - dx) % 4), ((4 - dx) % 4, (4 - dy) % 4), ((4 - dy) % 4, dx))[turn_by]
            children = lookup(CHILDREN, 4 * u + v)
            depth = lookup(DEPTH, 4 * u + v)
            has = [(children // (1 << e)) % 2 == 1 for e in range(4)]
            first = jnp.where(children > 0, TREE * depth, NEVER)
            flows.append((turn_by, has, depth > 0, first, children > 0))
    sides = (4 * y + (x + 1) % 4, 4 * ((y + 1) % 4) + x, 4 * y + (x + 3) % 4, 4 * ((y + 3) % 4) + x)

    barrier = pltpu.get_barrier_semaphore()

    def greet(pp, qq):
        pl.semaphore_signal(
            barrier, inc=1, device_id={"prow": pp, "pcol": qq}, device_id_type=pl.DeviceIdType.MESH
        )

    def greet_column(i, _):
        greet((p + i) % 8, q)
        return 0

    def greet_plane(i, _):
        greet(p, (q + i) % 16)
        return 0

    def greet_dest(i, _):
        other = (q + i) % 16

        @pl.when(i != 8)
        def _():
            greet(other % 8, other)

        return 0

    lax.fori_loop(1, 8, greet_column, 0)
    lax.fori_loop(1, 16, greet_plane, 0)

    @pl.when(is_dest)
    def _():
        lax.fori_loop(1, 16, greet_dest, 0)

    def turn_panel(panel):
        load_l(panel).wait()

        def turn(kb, _):
            hi, lo = split(lbuf[panel, kb].T)
            at = pl.ds(pl.multiple_of(kb * B, B), B)
            lthi[panel * B:(panel + 1) * B, at] = hi
            ltlo[panel * B:(panel + 1) * B, at] = lo
            return 0

        lax.fori_loop(0, 8, turn, 0)

    turn_panel(0)

    @pl.when(is_dest)
    def _():
        pl.semaphore_wait(barrier, 36)

    @pl.when(jnp.logical_not(is_dest))
    def _():
        pl.semaphore_wait(barrier, 22)

    corner = remote(l1_hbm.at[0, 0], kbuf, ksend, krecv, home, q)
    corner_here = pltpu.make_async_copy(l1_hbm.at[0, 0], kbuf, krecv)

    @pl.when(jnp.logical_and(p == 0, jnp.logical_not(is_dest)))
    def _():
        corner.start()

    @pl.when(jnp.logical_and(p == 0, is_dest))
    def _():
        corner_here.start()

    def swap_whole(n):
        return remote(pbuf.at[n], xbuf.at[n], xsend.at[n], xrecv.at[n], 2 * z + cd, q)

    def swap_half(n):
        rows = pl.ds(pl.multiple_of((1 - c) * HALF, HALF), HALF)
        return remote(
            pbuf.at[n, rows], xbuf.at[n, pl.ds(0, HALF)], xsend.at[n], xrecv.at[n], 2 * z + 1 - c, q
        )

    def products(n):
        col = (n + 1) % 4
        panel = n // 4

        @pl.when(n < 4)
        def _():
            load_g(col).wait()

            def halve(kb, _):
                hi, lo = split(gbuf[col, kb])
                at = pl.ds(pl.multiple_of(kb * B, B), B)
                ghi[col, at, :] = hi
                glo[col, at, :] = lo
                return 0

            lax.fori_loop(0, 8, halve, 0)

        rows = pl.ds(pl.multiple_of(panel * B, B), B)
        lh = lthi[rows, :]
        pbuf[n] = mm(lh, ghi[col]) + (mm(lh, glo[col]) + mm(ltlo[rows, :], ghi[col]))

        @pl.when(helper)
        def _():
            swap_whole(n).start()

        @pl.when(off_chip)
        def _():
            swap_half(n).start()

    def pass_on(n):
        last = pos == 2
        zn = jnp.where(c == 0, (z + 1) % 4, (z + 3) % 4)
        cn = jnp.where(last, cd, c)
        return remote(sbuf.at[n], cbuf.at[n, c], csend.at[n], crecv.at[n, c], 2 * zn + cn, q)

    def got_sum(n, half):
        return remote(cbuf.at[n, half], cbuf.at[n, half], csend.at[n], crecv.at[n, half], home, q)

    def chain(n):
        swap_half(n).wait_recv()
        rows = pl.ds(pl.multiple_of(c * HALF, HALF), HALF)
        sbuf[n] = pbuf[n, rows, :] + xbuf[n, 0:HALF, :]

        @pl.when(pos > 0)
        def _():
            got_sum(n, c).wait_recv()
            sbuf[n] += cbuf[n, c]

        pass_on(n).start()

    def whole_sum(n):
        swap_whole(n).wait_recv()
        got_sum(n, 0).wait_recv()
        got_sum(n, 1).wait_recv()
        xbuf[n] += pbuf[n]
        xbuf[n, 0:HALF, :] += cbuf[n, 0]
        xbuf[n, HALF:B, :] += cbuf[n, 1]
        return xbuf[n]

    def keep_turned(i, value):
        hi, lo = split(value.T)
        turned_hi[i] = hi
        turned_lo[i] = lo

    def turned_dot3(i, right):
        rh, rl = split(right)
        lh = turned_hi[i]
        return mm(lh, rh) + (mm(lh, rl) + mm(turned_lo[i], rh))

    def finish_two(n):
        col = (n + 1) % 4
        r = 2 * col + q // 8
        total = whole_sum(n)
        load_h(0, col).wait()
        resid = hbuf[0, col].T - 2.0 * total
        at = turned_dot3(0, resid)
        obuf[pl.ds(8 * n + 4 * (q // 8), 4)] = at.T.reshape(4, QUARTER, B)
        atbuf[n] = at

    def sums_two(n):
        col = (n + 1) % 4
        r = 2 * col + q // 8
        at = atbuf[n]
        dacc2[:, 0:16, :] += dot3(at, lbuf[0, r]).reshape(16, 16, B)
        dacc2[:, 16:32, :] += dot3(at, lbuf[1, r]).reshape(16, 16, B)
        zbuf[col] = SCALE * turned_dot3(2, at)

    def finish_one(n):
        col = (n + 1) % 4
        r = 2 * col + q // 8
        total = whole_sum(n)
        load_h(1, col).wait()
        resid = hbuf[1, col].T - 2.0 * total - zbuf[col]
        xbuf[n] = resid

        @pl.when(jnp.logical_and(is_root, n == 7))
        def _():
            def got(i, _):
                cross_rows(i).wait_recv()
                return 0

            lax.fori_loop(1, 16, got, 0)
            xbuf[n] -= xfull[...].T

        at = turned_dot3(1, xbuf[n])
        obuf[pl.ds(8 * n + 4 * (q // 8), 4)] = at.T.reshape(4, QUARTER, B)
        atbuf[n] = at

    def sums_one(n):
        r = 2 * ((n + 1) % 4) + q // 8
        dacc1[...] += dot3(atbuf[n], lbuf[1, r]).reshape(16, 16, B)

    def rows16(j):
        return pl.ds(pl.multiple_of((2 * (j % 8) + j // 8) * 16, 16), 16)

    def spread(rnd, j, me):
        src, dst = ((dacc2, rs2), (dacc1, rs1))[rnd]
        return remote(
            src.at[2 * (j % 8) + j // 8], dst.at[me], rsend.at[rnd, j], rrecv.at[rnd, me], j % 8, j
        )

    def spread_all(rnd):
        def send(i, _):
            spread(rnd, (q + i) % 16, q).start()
            return 0

        lax.fori_loop(1, 16, send, 0)

    def cross_rows(j):
        return remote(xfull.at[rows16(j)], xfull.at[rows16(j)], xxsend, xxrecv.at[j], 0, 0)

    def to_plane(rnd, i, h):
        mine = dfull.at[rnd, rows16(p + 8 * h)]
        return remote(mine, mine, bsend.at[rnd, i], brecv.at[rnd, h], p, (q + i) % 16)

    def own_rows(rnd):
        src, dst = ((dacc2, rs2), (dacc1, rs1))[rnd]

        def add(i, acc):
            j = (q + i) % 16
            spread(rnd, q, j).wait_recv()
            return acc + dst[j]

        total = lax.fori_loop(1, 16, add, src[2 * (q % 8) + q // 8])
        dfull[rnd, rows16(q), :] = -SCALE * total[0:16]
        if rnd == 0:
            xfull[rows16(q), :] = SCALE * total[16:32]

            @pl.when(jnp.logical_not(is_root))
            def _():
                cross_rows(q).start()

        def send(i, _):
            to_plane(rnd, i, q // 8).start()
            return 0

        lax.fori_loop(1, 16, send, 0)

    def pair_rows(rnd, pp, i):
        here = dfull.at[rnd, pl.ds(pl.multiple_of(pp * 32, 32), 32)]
        return remote(here, here, vsend.at[rnd, i], drecv.at[rnd, pp], (p + i) % 8, q)

    def to_column(rnd):
        for h in range(2):
            @pl.when(p + 8 * h != q)
            def _(h=h):
                to_plane(rnd, 1, h).wait_recv()

        def send(i, _):
            pair_rows(rnd, p, i).start()
            return 0

        lax.fori_loop(1, 8, send, 0)

    def branch(n, f, e):
        part = obuf.at[8 * n + f]
        return remote(
            part, part, tsend.at[n, f, e], trecv.at[8 * n + f], p, sides[(e + flows[f][0]) % 4]
        )

    def store(n):
        for f in range(8):
            @pl.when(jnp.logical_not(flows[f][4]))
            def _(f=f):
                branch(n, f, 0).wait_recv()

        for h in range(2):
            r = 2 * ((n + 1) % 4) + h
            tile = obuf.at[pl.ds(8 * n + 4 * h, 4)]

            @pl.when(n < 4)
            def _(r=r, tile=tile):
                pltpu.make_async_copy(tile, a2_hbm.at[r], osem.at[0]).start()

            @pl.when(n >= 4)
            def _(r=r, tile=tile):
                pltpu.make_async_copy(tile, a1_hbm.at[r], osem.at[1]).start()

    def forward(since, f):
        _, has, below, first, _ = flows[f]
        n = since - first

        @pl.when(jnp.logical_and(n >= 0, n < BLOCKS))
        def _():
            @pl.when(below)
            def _():
                branch(n, f, 0).wait_recv()

            for e in range(4):
                @pl.when(has[e])
                def _(e=e):
                    branch(n, f, e).start()

    def chain_turn(t):
        ahead = t - 1 - HOP * pos

        @pl.when(jnp.logical_and(off_chip, jnp.logical_and(ahead >= 0, ahead < BLOCKS)))
        def _():
            chain(ahead)

    def columns(since):
        for rnd in range(2):
            @pl.when(since == COLUMN[rnd])
            def _(rnd=rnd):
                to_column(rnd)

    def pass_all(since):
        for f in range(8):
            forward(since, f)

    def produce(t, _):
        products(t)

        @pl.when(t == 3)
        def _():
            turn_panel(1)

        chain_turn(t)
        return 0

    lax.fori_loop(0, BLOCKS, produce, 0)

    def pass_sums(t, _):
        chain_turn(t)
        return 0

    lax.fori_loop(BLOCKS, START, pass_sums, 0)

    @pl.when(is_dest)
    def _():
        dacc2[...] = jnp.zeros_like(dacc2)
        dacc1[...] = jnp.zeros_like(dacc1)
        keep_turned(0, w2_ref[...])
        keep_turned(1, w1_ref[...])
        corner_here.wait()
        keep_turned(2, kbuf[...])

    def finish_step(since, _):
        chain_turn(START + since)

        def finish(n, _):
            @pl.when(n < 4)
            def _():
                finish_two(n)

            @pl.when(n >= 4)
            def _():
                finish_one(n)

            return 0

        def sums(n, _):
            @pl.when(n < 4)
            def _():
                sums_two(n)

            @pl.when(n >= 4)
            def _():
                sums_one(n)

            return 0

        before = lookup((0,) + FINISHED, since)
        after = lookup(FINISHED, since)

        @pl.when(is_dest)
        def _():
            lax.fori_loop(before, after, finish, 0)

        pass_all(since)

        @pl.when(is_dest)
        def _():
            lax.fori_loop(before, after, sums, 0)

            for rnd in range(2):
                @pl.when(since == SPREAD[rnd])
                def _(rnd=rnd):
                    spread_all(rnd)

            @pl.when(since == OWN[0])
            def _():
                own_rows(0)

        return 0

    lax.fori_loop(0, len(FINISHED), finish_step, 0)

    def last_step(since, _):
        pass_all(since)

        @pl.when(jnp.logical_and(is_dest, since == OWN[1]))
        def _():
            own_rows(1)

        columns(since)
        complete = since - TREE * DEEPEST

        @pl.when(complete >= 0)
        def _():
            store(complete)

        return 0

    lax.fori_loop(len(FINISHED), LAST + 1, last_step, 0)

    for rnd, out in ((0, d2_hbm), (1, d1_hbm)):
        def late(i, _, rnd=rnd):
            pair_rows(rnd, (p + i) % 8, 0).wait_recv()
            return 0

        lax.fori_loop(1, 8, late, 0)
        pltpu.make_async_copy(dfull.at[rnd], out, osem.at[2 + rnd]).start()

    def sent(n, _):
        @pl.when(helper)
        def _():
            swap_whole(n).wait_send()

        @pl.when(off_chip)
        def _():
            swap_half(n).wait_send()
            pass_on(n).wait_send()

        return 0

    lax.fori_loop(0, BLOCKS, sent, 0)

    @pl.when(jnp.logical_and(p == 0, jnp.logical_not(is_dest)))
    def _():
        corner.wait_send()

    for f in range(8):
        for e in range(4):
            @pl.when(flows[f][1][e])
            def _(f=f, e=e):
                def part_sent(n, _):
                    branch(n, f, e).wait_send()
                    return 0

                lax.fori_loop(0, BLOCKS, part_sent, 0)

    for rnd in range(2):
        def column_sent(i, _, rnd=rnd):
            pair_rows(rnd, p, i).wait_send()
            return 0

        lax.fori_loop(1, 8, column_sent, 0)

        @pl.when(is_dest)
        def _(rnd=rnd):
            def home_sent(i, _):
                spread(rnd, (q + i) % 16, q).wait_send()
                to_plane(rnd, i, q // 8).wait_send()
                return 0

            lax.fori_loop(1, 16, home_sent, 0)

    @pl.when(jnp.logical_and(is_dest, jnp.logical_not(is_root)))
    def _():
        cross_rows(q).wait_send()

    pltpu.make_async_copy(a2_hbm, a2_hbm, osem.at[0]).wait()
    pltpu.make_async_copy(a1_hbm, a1_hbm, osem.at[1]).wait()
    pltpu.make_async_copy(dfull.at[0], d2_hbm, osem.at[2]).wait()
    pltpu.make_async_copy(dfull.at[1], d1_hbm, osem.at[3]).wait()


def hand_over(a1_in, a2_in, d1_in, d2_in, a1_out, a2_out, d1_out, d2_out, tiles, squares, sem_in, sem_out):
    moves = []
    for r in range(8):
        moves.append((a1_in.at[r, 0], tiles.at[0, r], a1_out.at[r, 0]))
        moves.append((a2_in.at[r, 0], tiles.at[1, r], a2_out.at[r, 0]))
    moves.append((d1_in, squares.at[0], d1_out))
    moves.append((d2_in, squares.at[1], d2_out))
    loads = [pltpu.make_async_copy(src, mid, sem_in.at[i]) for i, (src, mid, _) in enumerate(moves)]
    stores = [pltpu.make_async_copy(mid, dst, sem_out.at[i]) for i, (_, mid, dst) in enumerate(moves)]
    for load in loads:
        load.start()
    for load, store in zip(loads, stores):
        load.wait()
        store.start()
    for store in stores:
        store.wait()


def local(grad_trailing, panel_one, panel_two, grad_one, grad_two, inv_one, inv_two):
    any_space = pl.BlockSpec(memory_space=pl.ANY)
    vmem = pl.BlockSpec(memory_space=pltpu.VMEM)
    panel = jax.ShapeDtypeStruct(panel_one.shape, F32)
    grouped = jax.ShapeDtypeStruct((8, 4, QUARTER, B), F32)
    square = jax.ShapeDtypeStruct((B, B), F32)
    dma = pltpu.SemaphoreType.DMA
    results = pl.pallas_call(
        kernel,
        out_shape=(grouped, grouped, square, square),
        in_specs=[any_space] * 5 + [vmem] * 2,
        out_specs=(any_space,) * 4,
        scratch_shapes=[
            pltpu.VMEM((4, 8, B, B), F32),
            pltpu.VMEM((4, 8 * B, B), BF16),
            pltpu.VMEM((4, 8 * B, B), BF16),
            pltpu.VMEM((3, B, B), BF16),
            pltpu.VMEM((3, B, B), BF16),
            pltpu.VMEM((2, 8, B, B), F32),
            pltpu.VMEM((2 * B, 8 * B), BF16),
            pltpu.VMEM((2 * B, 8 * B), BF16),
            pltpu.VMEM((2, 4, B, B), F32),
            pltpu.VMEM((B, B), F32),
            pltpu.VMEM((4, B, B), F32),
            pltpu.VMEM((BLOCKS, B, B), F32),
            pltpu.VMEM((BLOCKS, B, B), F32),
            pltpu.VMEM((BLOCKS, 2, HALF, B), F32),
            pltpu.VMEM((BLOCKS, HALF, B), F32),
            pltpu.VMEM((8 * BLOCKS, QUARTER, B), F32),
            pltpu.VMEM((BLOCKS, B, B), F32),
            pltpu.VMEM((16, 32, B), F32),
            pltpu.VMEM((16, 16, B), F32),
            pltpu.VMEM((16, 32, B), F32),
            pltpu.VMEM((16, 16, B), F32),
            pltpu.VMEM((2, B, B), F32),
            pltpu.VMEM((B, B), F32),
            dma((4,)),
            dma((2,)),
            dma((2, 4)),
            dma,
            dma,
            dma((BLOCKS,)),
            dma((BLOCKS,)),
            dma((BLOCKS,)),
            dma((BLOCKS, 2)),
            dma((BLOCKS, 8, 4)),
            dma((BLOCKS * 8,)),
            dma((4,)),
            dma((2, 16)),
            dma((2, 16)),
            dma((2, 16)),
            dma((2, 2)),
            dma((2, 8)),
            dma((2, 8)),
            dma,
            dma((16,)),
        ],
        compiler_params=pltpu.CompilerParams(
            collective_id=0, has_side_effects=True, vmem_limit_bytes=56 * 2**20
        ),
        cost_estimate=pl.CostEstimate(flops=7_000_000_000, bytes_accessed=22_000_000, transcendentals=0),
    )(grad_trailing, panel_one, panel_two, grad_one, grad_two, inv_one, inv_two)
    return pl.pallas_call(
        hand_over,
        out_shape=(panel, panel, square, square),
        in_specs=[any_space] * 4,
        out_specs=(any_space,) * 4,
        scratch_shapes=[
            pltpu.VMEM((2, 8, B, B), F32),
            pltpu.VMEM((2, B, B), F32),
            dma((18,)),
            dma((18,)),
        ],
        compiler_params=pltpu.CompilerParams(vmem_limit_bytes=16 * 2**20),
    )(results[0].reshape(panel.shape), results[1].reshape(panel.shape), *results[2:])


def solution(mesh):
    placed = (
        P(None, "prow", None, None, "pcol", None),
        P(None, "prow", None, None),
        P(None, "prow", None, None),
        P(None, "prow", None, None),
        P(None, "prow", None, None),
        P(),
        P(),
    )
    return jax.shard_map(
        local,
        mesh=mesh,
        in_specs=placed,
        out_specs=(P(None, "prow", None, None), P(None, "prow", None, None), P(), P()),
        check_vma=False,
    )
```

```python
import math

import jax
import jax.numpy as jnp
from jax import lax
from jax.experimental import pallas as pl
from jax.experimental.pallas import tpu as pltpu
from jax.sharding import PartitionSpec as P

N = 16384
B = 256
HALF = B // 2
QUARTER = B // 4
SCALE = 1.0 / math.sqrt(N)
F32 = jnp.float32
BF16 = jnp.bfloat16

CHILDREN = (1, 0, 0, 0, 11, 7, 5, 4, 9, 1, 1, 1, 0, 0, 0, 0)
DEPTH = (0, 3, 4, 3, 1, 2, 3, 2, 2, 3, 4, 3, 3, 4, 5, 4)
DEEPEST = max(DEPTH)
BLOCKS = 8
HOP = 2
START = 2 + 3 * HOP
TREE = 2
SPREAD = (3, 7)
OWN = (5, 10)
COLUMN = (8, 13)
LAST = BLOCKS - 1 + TREE * DEEPEST
NEVER = 1 << 20


def split(value):
    high = value.astype(BF16)
    return high, (value - high.astype(F32)).astype(BF16)


def mm(left, right):
    return jnp.dot(left, right, preferred_element_type=F32)


def dot3(left, right):
    lh, ll = split(left)
    rh, rl = split(right)
    return mm(lh, rh) + (mm(lh, rl) + mm(ll, rh))


def lookup(table, index):
    found = jnp.int32(table[0])
    for at in range(1, len(table)):
        found = jnp.where(index == at, jnp.int32(table[at]), found)
    return found


def kernel(
    g_hbm, l1_hbm, l2_hbm, h1_hbm, h2_hbm, w1_ref, w2_ref,
    a1_hbm, a2_hbm, d1_hbm, d2_hbm,
    gbuf, ghi, glo, turned_hi, turned_lo, lbuf, lthi, ltlo, hbuf, kbuf, zbuf, pbuf, xbuf, cbuf, sbuf, obuf, atbuf,
    dacc2, dacc1, rs2, rs1, dfull, xfull,
    gsem, lsem, hsem, ksend, krecv, xsend, xrecv, csend, crecv, tsend, trecv, osem,
    rsend, rrecv, bsend, brecv, drecv, vsend, xxsend, xxrecv,
):
    p = lax.axis_index("prow")
    q = lax.axis_index("pcol")
    z, c = p // 2, p % 2
    y, x = q // 4, q % 4
    zd, cd = (q % 8) // 2, q % 2
    k = (z - zd + 4) % 4
    off_chip = k != 0
    is_dest = q % 8 == p
    helper = jnp.logical_and(k == 0, c != cd)
    pos = jnp.where(c == 0, k - 1, 3 - k)
    home = 2 * zd + cd
    is_root = jnp.logical_and(p == 0, q == 0)

    def remote(src, dst, send, recv, pp, qq):
        return pltpu.make_async_remote_copy(
            src_ref=src, dst_ref=dst, send_sem=send, recv_sem=recv,
            device_id={"prow": pp, "pcol": qq}, device_id_type=pl.DeviceIdType.MESH,
        )

    def load_l(panel):
        src = (l2_hbm, l1_hbm)[panel]
        return pltpu.make_async_copy(src.at[:, 0], lbuf.at[panel], lsem.at[panel])

    def load_g(col):
        return pltpu.make_async_copy(g_hbm.at[:, 0, :, col, 0, :], gbuf.at[col], gsem.at[col])

    def load_h(panel, col):
        src = (h2_hbm, h1_hbm)[panel]
        return pltpu.make_async_copy(src.at[2 * col + q // 8, 0], hbuf.at[panel, col], hsem.at[panel, col])

    load_l(0).start()
    load_l(1).start()
    for i in range(4):
        load_g((i + 1) % 4).start()

    @pl.when(is_dest)
    def _():
        for panel in range(2):
            for i in range(4):
                load_h(panel, (i + 1) % 4).start()

    flows = []
    for h in range(2):
        qs = p + 8 * h
        dx = (x - qs % 4 + 4) % 4
        dy = (y - qs // 4 + 4) % 4
        for turn_by in range(4):
            u, v = ((dx, dy), (dy, (4 - dx) % 4), ((4 - dx) % 4, (4 - dy) % 4), ((4 - dy) % 4, dx))[turn_by]
            children = lookup(CHILDREN, 4 * u + v)
            depth = lookup(DEPTH, 4 * u + v)
            has = [(children // (1 << e)) % 2 == 1 for e in range(4)]
            first = jnp.where(jnp.logical_and(children > 0, depth > 0), TREE * depth, NEVER)
            flows.append((turn_by, has, first, children > 0))
    sides = (4 * y + (x + 1) % 4, 4 * ((y + 1) % 4) + x, 4 * y + (x + 3) % 4, 4 * ((y + 3) % 4) + x)

    barrier = pltpu.get_barrier_semaphore()

    def greet(pp, qq):
        pl.semaphore_signal(
            barrier, inc=1, device_id={"prow": pp, "pcol": qq}, device_id_type=pl.DeviceIdType.MESH
        )

    def greet_column(i, _):
        greet((p + i) % 8, q)
        return 0

    def greet_plane(i, _):
        greet(p, (q + i) % 16)
        return 0

    def greet_dest(i, _):
        other = (q + i) % 16

        @pl.when(i != 8)
        def _():
            greet(other % 8, other)

        return 0

    lax.fori_loop(1, 8, greet_column, 0)
    lax.fori_loop(1, 16, greet_plane, 0)

    @pl.when(is_dest)
    def _():
        lax.fori_loop(1, 16, greet_dest, 0)

    def turn_panel(panel):
        load_l(panel).wait()

        def turn(kb, _):
            hi, lo = split(lbuf[panel, kb].T)
            at = pl.ds(pl.multiple_of(kb * B, B), B)
            lthi[panel * B:(panel + 1) * B, at] = hi
            ltlo[panel * B:(panel + 1) * B, at] = lo
            return 0

        lax.fori_loop(0, 8, turn, 0)

    turn_panel(0)

    @pl.when(is_dest)
    def _():
        pl.semaphore_wait(barrier, 36)

    @pl.when(jnp.logical_not(is_dest))
    def _():
        pl.semaphore_wait(barrier, 22)

    corner = remote(l1_hbm.at[0, 0], kbuf, ksend, krecv, home, q)
    corner_here = pltpu.make_async_copy(l1_hbm.at[0, 0], kbuf, krecv)

    @pl.when(jnp.logical_and(p == 0, jnp.logical_not(is_dest)))
    def _():
        corner.start()

    @pl.when(jnp.logical_and(p == 0, is_dest))
    def _():
        corner_here.start()

    def swap_whole(n):
        return remote(pbuf.at[n], xbuf.at[n], xsend.at[n], xrecv.at[n], 2 * z + cd, q)

    def swap_half(n):
        rows = pl.ds(pl.multiple_of((1 - c) * HALF, HALF), HALF)
        return remote(
            pbuf.at[n, rows], xbuf.at[n, pl.ds(0, HALF)], xsend.at[n], xrecv.at[n], 2 * z + 1 - c, q
        )

    def products(n):
        col = (n + 1) % 4
        panel = n // 4

        @pl.when(n < 4)
        def _():
            load_g(col).wait()

            def halve(kb, _):
                hi, lo = split(gbuf[col, kb])
                at = pl.ds(pl.multiple_of(kb * B, B), B)
                ghi[col, at, :] = hi
                glo[col, at, :] = lo
                return 0

            lax.fori_loop(0, 8, halve, 0)

        rows = pl.ds(pl.multiple_of(panel * B, B), B)
        lh = lthi[rows, :]
        pbuf[n] = mm(lh, ghi[col]) + (mm(lh, glo[col]) + mm(ltlo[rows, :], ghi[col]))

        @pl.when(helper)
        def _():
            swap_whole(n).start()

        @pl.when(off_chip)
        def _():
            swap_half(n).start()

    def pass_on(n):
        last = pos == 2
        zn = jnp.where(c == 0, (z + 1) % 4, (z + 3) % 4)
        cn = jnp.where(last, cd, c)
        return remote(sbuf.at[n], cbuf.at[n, c], csend.at[n], crecv.at[n, c], 2 * zn + cn, q)

    def got_sum(n, half):
        return remote(cbuf.at[n, half], cbuf.at[n, half], csend.at[n], crecv.at[n, half], home, q)

    def chain(n):
        swap_half(n).wait_recv()
        rows = pl.ds(pl.multiple_of(c * HALF, HALF), HALF)
        sbuf[n] = pbuf[n, rows, :] + xbuf[n, 0:HALF, :]

        @pl.when(pos > 0)
        def _():
            got_sum(n, c).wait_recv()
            sbuf[n] += cbuf[n, c]

        pass_on(n).start()

    def whole_sum(n):
        swap_whole(n).wait_recv()
        got_sum(n, 0).wait_recv()
        got_sum(n, 1).wait_recv()
        xbuf[n] += pbuf[n]
        xbuf[n, 0:HALF, :] += cbuf[n, 0]
        xbuf[n, HALF:B, :] += cbuf[n, 1]
        return xbuf[n]

    def keep_turned(i, value):
        hi, lo = split(value.T)
        turned_hi[i] = hi
        turned_lo[i] = lo

    def turned_dot3(i, right):
        rh, rl = split(right)
        lh = turned_hi[i]
        return mm(lh, rh) + (mm(lh, rl) + mm(turned_lo[i], rh))

    def finish_two(n):
        col = (n + 1) % 4
        r = 2 * col + q // 8
        total = whole_sum(n)
        resid = hbuf[0, col] - 2.0 * total
        at = turned_dot3(0, resid)
        obuf[pl.ds(8 * n + 4 * (q // 8), 4)] = at.T.reshape(4, QUARTER, B)
        atbuf[n] = at

    def sums_two(n):
        col = (n + 1) % 4
        r = 2 * col + q // 8
        at = atbuf[n]
        dacc2[:, 0:16, :] += dot3(at, lbuf[0, r]).reshape(16, 16, B)
        dacc2[:, 16:32, :] += dot3(at, lbuf[1, r]).reshape(16, 16, B)
        zbuf[col] = SCALE * turned_dot3(2, at)

    def finish_one(n):
        col = (n + 1) % 4
        r = 2 * col + q // 8
        total = whole_sum(n)
        resid = hbuf[1, col] - 2.0 * total - zbuf[col]
        xbuf[n] = resid

        @pl.when(jnp.logical_and(is_root, n == 7))
        def _():
            def got(i, _):
                cross_rows(i).wait_recv()
                return 0

            lax.fori_loop(1, 16, got, 0)
            xbuf[n] -= xfull[...].T

        at = turned_dot3(1, xbuf[n])
        obuf[pl.ds(8 * n + 4 * (q // 8), 4)] = at.T.reshape(4, QUARTER, B)
        atbuf[n] = at

    def sums_one(n):
        r = 2 * ((n + 1) % 4) + q // 8
        dacc1[...] += dot3(atbuf[n], lbuf[1, r]).reshape(16, 16, B)

    def rows16(j):
        return pl.ds(pl.multiple_of((2 * (j % 8) + j // 8) * 16, 16), 16)

    def spread(rnd, j, me):
        src, dst = ((dacc2, rs2), (dacc1, rs1))[rnd]
        return remote(
            src.at[2 * (j % 8) + j // 8], dst.at[me], rsend.at[rnd, j], rrecv.at[rnd, me], j % 8, j
        )

    def spread_all(rnd):
        def send(i, _):
            spread(rnd, (q + i) % 16, q).start()
            return 0

        lax.fori_loop(1, 16, send, 0)

    def cross_rows(j):
        return remote(xfull.at[rows16(j)], xfull.at[rows16(j)], xxsend, xxrecv.at[j], 0, 0)

    def to_plane(rnd, i, h):
        mine = dfull.at[rnd, rows16(p + 8 * h)]
        return remote(mine, mine, bsend.at[rnd, i], brecv.at[rnd, h], p, (q + i) % 16)

    def own_rows(rnd):
        src, dst = ((dacc2, rs2), (dacc1, rs1))[rnd]

        def add(i, acc):
            j = (q + i) % 16
            spread(rnd, q, j).wait_recv()
            return acc + dst[j]

        total = lax.fori_loop(1, 16, add, src[2 * (q % 8) + q // 8])
        dfull[rnd, rows16(q), :] = -SCALE * total[0:16]
        if rnd == 0:
            xfull[rows16(q), :] = SCALE * total[16:32]

            @pl.when(jnp.logical_not(is_root))
            def _():
                cross_rows(q).start()

        def send(i, _):
            to_plane(rnd, i, q // 8).start()
            return 0

        lax.fori_loop(1, 16, send, 0)

    def pair_rows(rnd, pp, i):
        here = dfull.at[rnd, pl.ds(pl.multiple_of(pp * 32, 32), 32)]
        return remote(here, here, vsend.at[rnd, i], drecv.at[rnd, pp], (p + i) % 8, q)

    def to_column(rnd):
        for h in range(2):
            @pl.when(p + 8 * h != q)
            def _(h=h):
                to_plane(rnd, 1, h).wait_recv()

        def send(i, _):
            pair_rows(rnd, p, i).start()
            return 0

        lax.fori_loop(1, 8, send, 0)

    def branch(n, f, e):
        part = obuf.at[8 * n + f]
        return remote(
            part, part, tsend.at[n, f, e], trecv.at[8 * n + f], p, sides[(e + flows[f][0]) % 4]
        )

    def store(n):
        for f in range(8):
            @pl.when(jnp.logical_not(flows[f][3]))
            def _(f=f):
                branch(n, f, 0).wait_recv()

        for h in range(2):
            r = 2 * ((n + 1) % 4) + h
            tile = obuf.at[pl.ds(8 * n + 4 * h, 4)]

            @pl.when(n < 4)
            def _(r=r, tile=tile):
                pltpu.make_async_copy(tile, a2_hbm.at[r], osem.at[0]).start()

            @pl.when(n >= 4)
            def _(r=r, tile=tile):
                pltpu.make_async_copy(tile, a1_hbm.at[r], osem.at[1]).start()

    def set_out(n):
        for turn_by in range(4):
            f = 4 * (q // 8) + turn_by
            part = obuf.at[8 * n + f]
            remote(part, part, tsend.at[n, f, 0], trecv.at[8 * n + f], p, sides[turn_by]).start()

    def forward(since, f):
        _, has, first, _ = flows[f]
        n = since - first

        @pl.when(jnp.logical_and(n >= 0, n < BLOCKS))
        def _():
            branch(n, f, 0).wait_recv()

            for e in range(4):
                @pl.when(has[e])
                def _(e=e):
                    branch(n, f, e).start()

    def chain_turn(t):
        ahead = t - 1 - HOP * pos

        @pl.when(jnp.logical_and(off_chip, jnp.logical_and(ahead >= 0, ahead < BLOCKS)))
        def _():
            chain(ahead)

    def columns(since):
        for rnd in range(2):
            @pl.when(since == COLUMN[rnd])
            def _(rnd=rnd):
                to_column(rnd)

    def pass_all(since):
        for f in range(8):
            forward(since, f)

    def produce(t, _):
        products(t)

        @pl.when(t == 3)
        def _():
            turn_panel(1)

        chain_turn(t)
        return 0

    lax.fori_loop(0, BLOCKS, produce, 0)

    def pass_sums(t, _):
        chain_turn(t)
        return 0

    lax.fori_loop(BLOCKS, START, pass_sums, 0)

    @pl.when(is_dest)
    def _():
        dacc2[...] = jnp.zeros_like(dacc2)
        dacc1[...] = jnp.zeros_like(dacc1)
        for panel in range(2):
            def turn_h(col, _, panel=panel):
                load_h(panel, col).wait()
                hbuf[panel, col] = hbuf[panel, col].T
                return 0

            lax.fori_loop(0, 4, turn_h, 0)
        keep_turned(0, w2_ref[...])
        keep_turned(1, w1_ref[...])
        corner_here.wait()
        keep_turned(2, kbuf[...])

    def finish_step(since, _):
        chain_turn(START + since)

        @pl.when(is_dest)
        def _():
            @pl.when(since < 4)
            def _():
                finish_two(since)

            @pl.when(since >= 4)
            def _():
                finish_one(since)

            set_out(since)

        pass_all(since)

        @pl.when(is_dest)
        def _():
            @pl.when(since < 4)
            def _():
                sums_two(since)

            @pl.when(since >= 4)
            def _():
                sums_one(since)

            for rnd in range(2):
                @pl.when(since == SPREAD[rnd])
                def _(rnd=rnd):
                    spread_all(rnd)

            @pl.when(since == OWN[0])
            def _():
                own_rows(0)

        return 0

    lax.fori_loop(0, BLOCKS, finish_step, 0)

    def last_step(since, _):
        pass_all(since)

        @pl.when(jnp.logical_and(is_dest, since == OWN[1]))
        def _():
            own_rows(1)

        columns(since)
        complete = since - TREE * DEEPEST

        @pl.when(complete >= 0)
        def _():
            store(complete)

        return 0

    lax.fori_loop(BLOCKS, LAST + 1, last_step, 0)

    for rnd, out in ((0, d2_hbm), (1, d1_hbm)):
        def late(i, _, rnd=rnd):
            pair_rows(rnd, (p + i) % 8, 0).wait_recv()
            return 0

        lax.fori_loop(1, 8, late, 0)
        pltpu.make_async_copy(dfull.at[rnd], out, osem.at[2 + rnd]).start()

    def sent(n, _):
        @pl.when(helper)
        def _():
            swap_whole(n).wait_send()

        @pl.when(off_chip)
        def _():
            swap_half(n).wait_send()
            pass_on(n).wait_send()

        return 0

    lax.fori_loop(0, BLOCKS, sent, 0)

    @pl.when(jnp.logical_and(p == 0, jnp.logical_not(is_dest)))
    def _():
        corner.wait_send()

    for f in range(8):
        for e in range(4):
            @pl.when(flows[f][1][e])
            def _(f=f, e=e):
                def part_sent(n, _):
                    branch(n, f, e).wait_send()
                    return 0

                lax.fori_loop(0, BLOCKS, part_sent, 0)

    for rnd in range(2):
        def column_sent(i, _, rnd=rnd):
            pair_rows(rnd, p, i).wait_send()
            return 0

        lax.fori_loop(1, 8, column_sent, 0)

        @pl.when(is_dest)
        def _(rnd=rnd):
            def home_sent(i, _):
                spread(rnd, (q + i) % 16, q).wait_send()
                to_plane(rnd, i, q // 8).wait_send()
                return 0

            lax.fori_loop(1, 16, home_sent, 0)

    @pl.when(jnp.logical_and(is_dest, jnp.logical_not(is_root)))
    def _():
        cross_rows(q).wait_send()

    pltpu.make_async_copy(a2_hbm, a2_hbm, osem.at[0]).wait()
    pltpu.make_async_copy(a1_hbm, a1_hbm, osem.at[1]).wait()
    pltpu.make_async_copy(dfull.at[0], d2_hbm, osem.at[2]).wait()
    pltpu.make_async_copy(dfull.at[1], d1_hbm, osem.at[3]).wait()


def hand_over(a1_in, a2_in, d1_in, d2_in, a1_out, a2_out, d1_out, d2_out, tiles, squares, sem_in, sem_out):
    moves = []
    for r in range(8):
        moves.append((a1_in.at[r, 0], tiles.at[0, r], a1_out.at[r, 0]))
        moves.append((a2_in.at[r, 0], tiles.at[1, r], a2_out.at[r, 0]))
    moves.append((d1_in, squares.at[0], d1_out))
    moves.append((d2_in, squares.at[1], d2_out))
    loads = [pltpu.make_async_copy(src, mid, sem_in.at[i]) for i, (src, mid, _) in enumerate(moves)]
    stores = [pltpu.make_async_copy(mid, dst, sem_out.at[i]) for i, (_, mid, dst) in enumerate(moves)]
    for load in loads:
        load.start()
    for load, store in zip(loads, stores):
        load.wait()
        store.start()
    for store in stores:
        store.wait()


def local(grad_trailing, panel_one, panel_two, grad_one, grad_two, inv_one, inv_two):
    any_space = pl.BlockSpec(memory_space=pl.ANY)
    vmem = pl.BlockSpec(memory_space=pltpu.VMEM)
    panel = jax.ShapeDtypeStruct(panel_one.shape, F32)
    grouped = jax.ShapeDtypeStruct((8, 4, QUARTER, B), F32)
    square = jax.ShapeDtypeStruct((B, B), F32)
    dma = pltpu.SemaphoreType.DMA
    results = pl.pallas_call(
        kernel,
        out_shape=(grouped, grouped, square, square),
        in_specs=[any_space] * 5 + [vmem] * 2,
        out_specs=(any_space,) * 4,
        scratch_shapes=[
            pltpu.VMEM((4, 8, B, B), F32),
            pltpu.VMEM((4, 8 * B, B), BF16),
            pltpu.VMEM((4, 8 * B, B), BF16),
            pltpu.VMEM((3, B, B), BF16),
            pltpu.VMEM((3, B, B), BF16),
            pltpu.VMEM((2, 8, B, B), F32),
            pltpu.VMEM((2 * B, 8 * B), BF16),
            pltpu.VMEM((2 * B, 8 * B), BF16),
            pltpu.VMEM((2, 4, B, B), F32),
            pltpu.VMEM((B, B), F32),
            pltpu.VMEM((4, B, B), F32),
            pltpu.VMEM((BLOCKS, B, B), F32),
            pltpu.VMEM((BLOCKS, B, B), F32),
            pltpu.VMEM((BLOCKS, 2, HALF, B), F32),
            pltpu.VMEM((BLOCKS, HALF, B), F32),
            pltpu.VMEM((8 * BLOCKS, QUARTER, B), F32),
            pltpu.VMEM((BLOCKS, B, B), F32),
            pltpu.VMEM((16, 32, B), F32),
            pltpu.VMEM((16, 16, B), F32),
            pltpu.VMEM((16, 32, B), F32),
            pltpu.VMEM((16, 16, B), F32),
            pltpu.VMEM((2, B, B), F32),
            pltpu.VMEM((B, B), F32),
            dma((4,)),
            dma((2,)),
            dma((2, 4)),
            dma,
            dma,
            dma((BLOCKS,)),
            dma((BLOCKS,)),
            dma((BLOCKS,)),
            dma((BLOCKS, 2)),
            dma((BLOCKS, 8, 4)),
            dma((BLOCKS * 8,)),
            dma((4,)),
            dma((2, 16)),
            dma((2, 16)),
            dma((2, 16)),
            dma((2, 2)),
            dma((2, 8)),
            dma((2, 8)),
            dma,
            dma((16,)),
        ],
        compiler_params=pltpu.CompilerParams(
            collective_id=0, has_side_effects=True, vmem_limit_bytes=56 * 2**20
        ),
        cost_estimate=pl.CostEstimate(flops=7_000_000_000, bytes_accessed=22_000_000, transcendentals=0),
    )(grad_trailing, panel_one, panel_two, grad_one, grad_two, inv_one, inv_two)
    return pl.pallas_call(
        hand_over,
        out_shape=(panel, panel, square, square),
        in_specs=[any_space] * 4,
        out_specs=(any_space,) * 4,
        scratch_shapes=[
            pltpu.VMEM((2, 8, B, B), F32),
            pltpu.VMEM((2, B, B), F32),
            dma((18,)),
            dma((18,)),
        ],
        compiler_params=pltpu.CompilerParams(vmem_limit_bytes=16 * 2**20),
    )(results[0].reshape(panel.shape), results[1].reshape(panel.shape), *results[2:])


def solution(mesh):
    placed = (
        P(None, "prow", None, None, "pcol", None),
        P(None, "prow", None, None),
        P(None, "prow", None, None),
        P(None, "prow", None, None),
        P(None, "prow", None, None),
        P(),
        P(),
    )
    return jax.shard_map(
        local,
        mesh=mesh,
        in_specs=placed,
        out_specs=(P(None, "prow", None, None), P(None, "prow", None, None), P(), P()),
        check_vma=False,
    )
```

```python
import math

import jax
import jax.numpy as jnp
from jax import lax
from jax.experimental import pallas as pl
from jax.experimental.pallas import tpu as pltpu
from jax.sharding import PartitionSpec as P

N = 16384
B = 256
HALF = B // 2
QUARTER = B // 4
SCALE = 1.0 / math.sqrt(N)
F32 = jnp.float32
BF16 = jnp.bfloat16

CHILDREN = (1, 0, 0, 0, 11, 7, 5, 4, 9, 1, 1, 1, 0, 0, 0, 0)
DEPTH = (0, 3, 4, 3, 1, 2, 3, 2, 2, 3, 4, 3, 3, 4, 5, 4)
DEEPEST = max(DEPTH)
BLOCKS = 8
HOP = 2
START = 2 + 3 * HOP
TREE = 2
SPREAD = (3, 7)
OWN = (5, 10)
COLUMN = (8, 13)
LAST = BLOCKS - 1 + TREE * DEEPEST
NEVER = 1 << 20


def split(value):
    high = value.astype(BF16)
    return high, (value - high.astype(F32)).astype(BF16)


def mm(left, right):
    return jnp.dot(left, right, preferred_element_type=F32)


def dot3(left, right):
    lh, ll = split(left)
    rh, rl = split(right)
    return mm(lh, rh) + (mm(lh, rl) + mm(ll, rh))


def lookup(table, index):
    found = jnp.int32(table[0])
    for at in range(1, len(table)):
        found = jnp.where(index == at, jnp.int32(table[at]), found)
    return found


def kernel(
    g_hbm, l1_hbm, l2_hbm, h1_hbm, h2_hbm, w1_ref, w2_ref,
    a1_hbm, a2_hbm, d1_hbm, d2_hbm,
    gbuf, ghi, glo, turned_hi, turned_lo, lbuf, lthi, ltlo, hbuf, kbuf, zbuf, pbuf, xbuf, cbuf, sbuf, obuf, atbuf,
    dacc2, dacc1, rs2, rs1, dfull, xfull,
    gsem, lsem, hsem, ksend, krecv, xsend, xrecv, csend, crecv, tsend, trecv, osem,
    rsend, rrecv, bsend, brecv, drecv, vsend, xxsend, xxrecv,
):
    p = lax.axis_index("prow")
    q = lax.axis_index("pcol")
    z, c = p // 2, p % 2
    y, x = q // 4, q % 4
    zd, cd = (q % 8) // 2, q % 2
    k = (z - zd + 4) % 4
    off_chip = k != 0
    is_dest = q % 8 == p
    helper = jnp.logical_and(k == 0, c != cd)
    pos = jnp.where(c == 0, k - 1, 3 - k)
    home = 2 * zd + cd
    is_root = jnp.logical_and(p == 0, q == 0)

    def remote(src, dst, send, recv, pp, qq):
        return pltpu.make_async_remote_copy(
            src_ref=src, dst_ref=dst, send_sem=send, recv_sem=recv,
            device_id={"prow": pp, "pcol": qq}, device_id_type=pl.DeviceIdType.MESH,
        )

    def load_l(panel):
        src = (l2_hbm, l1_hbm)[panel]
        return pltpu.make_async_copy(src.at[:, 0], lbuf.at[panel], lsem.at[panel])

    def load_g(col):
        return pltpu.make_async_copy(g_hbm.at[:, 0, :, col, 0, :], gbuf.at[col], gsem.at[col])

    def load_h(panel, col):
        src = (h2_hbm, h1_hbm)[panel]
        return pltpu.make_async_copy(src.at[2 * col + q // 8, 0], hbuf.at[panel, col], hsem.at[panel, col])

    load_l(0).start()
    for i in range(4):
        load_g((i + 1) % 4).start()
    load_l(1).start()

    @pl.when(is_dest)
    def _():
        for panel in range(2):
            for i in range(4):
                load_h(panel, (i + 1) % 4).start()

    flows = []
    for h in range(2):
        qs = p + 8 * h
        dx = (x - qs % 4 + 4) % 4
        dy = (y - qs // 4 + 4) % 4
        for turn_by in range(4):
            u, v = ((dx, dy), (dy, (4 - dx) % 4), ((4 - dx) % 4, (4 - dy) % 4), ((4 - dy) % 4, dx))[turn_by]
            children = lookup(CHILDREN, 4 * u + v)
            depth = lookup(DEPTH, 4 * u + v)
            has = [(children // (1 << e)) % 2 == 1 for e in range(4)]
            first = jnp.where(jnp.logical_and(children > 0, depth > 0), TREE * depth, NEVER)
            flows.append((turn_by, has, first, children > 0))
    sides = (4 * y + (x + 1) % 4, 4 * ((y + 1) % 4) + x, 4 * y + (x + 3) % 4, 4 * ((y + 3) % 4) + x)

    barrier = pltpu.get_barrier_semaphore()

    def greet(pp, qq):
        pl.semaphore_signal(
            barrier, inc=1, device_id={"prow": pp, "pcol": qq}, device_id_type=pl.DeviceIdType.MESH
        )

    def greet_column(i, _):
        greet((p + i) % 8, q)
        return 0

    def greet_plane(i, _):
        greet(p, (q + i) % 16)
        return 0

    def greet_dest(i, _):
        other = (q + i) % 16

        @pl.when(i != 8)
        def _():
            greet(other % 8, other)

        return 0

    lax.fori_loop(1, 8, greet_column, 0)
    lax.fori_loop(1, 16, greet_plane, 0)

    @pl.when(is_dest)
    def _():
        lax.fori_loop(1, 16, greet_dest, 0)

    def turn_panel(panel):
        load_l(panel).wait()

        def turn(kb, _):
            hi, lo = split(lbuf[panel, kb].T)
            at = pl.ds(pl.multiple_of(kb * B, B), B)
            lthi[panel * B:(panel + 1) * B, at] = hi
            ltlo[panel * B:(panel + 1) * B, at] = lo
            return 0

        lax.fori_loop(0, 8, turn, 0)

    turn_panel(0)

    @pl.when(is_dest)
    def _():
        pl.semaphore_wait(barrier, 36)

    @pl.when(jnp.logical_not(is_dest))
    def _():
        pl.semaphore_wait(barrier, 22)

    corner = remote(l1_hbm.at[0, 0], kbuf, ksend, krecv, home, q)
    corner_here = pltpu.make_async_copy(l1_hbm.at[0, 0], kbuf, krecv)

    @pl.when(jnp.logical_and(p == 0, jnp.logical_not(is_dest)))
    def _():
        corner.start()

    @pl.when(jnp.logical_and(p == 0, is_dest))
    def _():
        corner_here.start()

    def swap_whole(n):
        return remote(pbuf.at[n], xbuf.at[n], xsend.at[n], xrecv.at[n], 2 * z + cd, q)

    def swap_half(n):
        rows = pl.ds(pl.multiple_of((1 - c) * HALF, HALF), HALF)
        return remote(
            pbuf.at[n, rows], xbuf.at[n, pl.ds(0, HALF)], xsend.at[n], xrecv.at[n], 2 * z + 1 - c, q
        )

    def products(n):
        col = (n + 1) % 4
        panel = n // 4

        @pl.when(n < 4)
        def _():
            load_g(col).wait()

            def halve(kb, _):
                hi, lo = split(gbuf[col, kb])
                at = pl.ds(pl.multiple_of(kb * B, B), B)
                ghi[col, at, :] = hi
                glo[col, at, :] = lo
                return 0

            lax.fori_loop(0, 8, halve, 0)

        rows = pl.ds(pl.multiple_of(panel * B, B), B)
        lh = lthi[rows, :]
        pbuf[n] = mm(lh, ghi[col]) + (mm(lh, glo[col]) + mm(ltlo[rows, :], ghi[col]))

        @pl.when(helper)
        def _():
            swap_whole(n).start()

        @pl.when(off_chip)
        def _():
            swap_half(n).start()

    def pass_on(n):
        last = pos == 2
        zn = jnp.where(c == 0, (z + 1) % 4, (z + 3) % 4)
        cn = jnp.where(last, cd, c)
        return remote(sbuf.at[n], cbuf.at[n, c], csend.at[n], crecv.at[n, c], 2 * zn + cn, q)

    def got_sum(n, half):
        return remote(cbuf.at[n, half], cbuf.at[n, half], csend.at[n], crecv.at[n, half], home, q)

    def chain(n):
        swap_half(n).wait_recv()
        rows = pl.ds(pl.multiple_of(c * HALF, HALF), HALF)
        sbuf[n] = pbuf[n, rows, :] + xbuf[n, 0:HALF, :]

        @pl.when(pos > 0)
        def _():
            got_sum(n, c).wait_recv()
            sbuf[n] += cbuf[n, c]

        pass_on(n).start()

    def whole_sum(n):
        swap_whole(n).wait_recv()
        got_sum(n, 0).wait_recv()
        got_sum(n, 1).wait_recv()
        xbuf[n] += pbuf[n]
        xbuf[n, 0:HALF, :] += cbuf[n, 0]
        xbuf[n, HALF:B, :] += cbuf[n, 1]
        return xbuf[n]

    def keep_turned(i, value):
        hi, lo = split(value.T)
        turned_hi[i] = hi
        turned_lo[i] = lo

    def turned_dot3(i, right):
        rh, rl = split(right)
        lh = turned_hi[i]
        return mm(lh, rh) + (mm(lh, rl) + mm(turned_lo[i], rh))

    def finish_two(n):
        col = (n + 1) % 4
        r = 2 * col + q // 8
        total = whole_sum(n)
        resid = hbuf[0, col] - 2.0 * total
        at = turned_dot3(0, resid)
        obuf[pl.ds(8 * n + 4 * (q // 8), 4)] = at.T.reshape(4, QUARTER, B)
        atbuf[n] = at

    def sums_two(n):
        col = (n + 1) % 4
        r = 2 * col + q // 8
        at = atbuf[n]
        dacc2[:, 0:16, :] += dot3(at, lbuf[0, r]).reshape(16, 16, B)
        dacc2[:, 16:32, :] += dot3(at, lbuf[1, r]).reshape(16, 16, B)
        zbuf[col] = SCALE * turned_dot3(2, at)

    def finish_one(n):
        col = (n + 1) % 4
        r = 2 * col + q // 8
        total = whole_sum(n)
        resid = hbuf[1, col] - 2.0 * total - zbuf[col]
        xbuf[n] = resid

        @pl.when(jnp.logical_and(is_root, n == 7))
        def _():
            def got(i, _):
                cross_rows(i).wait_recv()
                return 0

            lax.fori_loop(1, 16, got, 0)
            xbuf[n] -= xfull[...].T

        at = turned_dot3(1, xbuf[n])
        obuf[pl.ds(8 * n + 4 * (q // 8), 4)] = at.T.reshape(4, QUARTER, B)
        atbuf[n] = at

    def sums_one(n):
        r = 2 * ((n + 1) % 4) + q // 8
        dacc1[...] += dot3(atbuf[n], lbuf[1, r]).reshape(16, 16, B)

    def rows16(j):
        return pl.ds(pl.multiple_of((2 * (j % 8) + j // 8) * 16, 16), 16)

    def spread(rnd, j, me):
        src, dst = ((dacc2, rs2), (dacc1, rs1))[rnd]
        return remote(
            src.at[2 * (j % 8) + j // 8], dst.at[me], rsend.at[rnd, j], rrecv.at[rnd, me], j % 8, j
        )

    def spread_all(rnd):
        def send(i, _):
            spread(rnd, (q + i) % 16, q).start()
            return 0

        lax.fori_loop(1, 16, send, 0)

    def cross_rows(j):
        return remote(xfull.at[rows16(j)], xfull.at[rows16(j)], xxsend, xxrecv.at[j], 0, 0)

    def to_plane(rnd, i, h):
        mine = dfull.at[rnd, rows16(p + 8 * h)]
        return remote(mine, mine, bsend.at[rnd, i], brecv.at[rnd, h], p, (q + i) % 16)

    def own_rows(rnd):
        src, dst = ((dacc2, rs2), (dacc1, rs1))[rnd]

        def add(i, acc):
            j = (q + i) % 16
            spread(rnd, q, j).wait_recv()
            return acc + dst[j]

        total = lax.fori_loop(1, 16, add, src[2 * (q % 8) + q // 8])
        dfull[rnd, rows16(q), :] = -SCALE * total[0:16]
        if rnd == 0:
            xfull[rows16(q), :] = SCALE * total[16:32]

            @pl.when(jnp.logical_not(is_root))
            def _():
                cross_rows(q).start()

        def send(i, _):
            to_plane(rnd, i, q // 8).start()
            return 0

        lax.fori_loop(1, 16, send, 0)

    def pair_rows(rnd, pp, i):
        here = dfull.at[rnd, pl.ds(pl.multiple_of(pp * 32, 32), 32)]
        return remote(here, here, vsend.at[rnd, i], drecv.at[rnd, pp], (p + i) % 8, q)

    def to_column(rnd):
        for h in range(2):
            @pl.when(p + 8 * h != q)
            def _(h=h):
                to_plane(rnd, 1, h).wait_recv()

        def send(i, _):
            pair_rows(rnd, p, i).start()
            return 0

        lax.fori_loop(1, 8, send, 0)

    def branch(n, f, e):
        part = obuf.at[8 * n + f]
        return remote(
            part, part, tsend.at[n, f, e], trecv.at[8 * n + f], p, sides[(e + flows[f][0]) % 4]
        )

    def store(n):
        for f in range(8):
            @pl.when(jnp.logical_not(flows[f][3]))
            def _(f=f):
                branch(n, f, 0).wait_recv()

        for h in range(2):
            r = 2 * ((n + 1) % 4) + h
            tile = obuf.at[pl.ds(8 * n + 4 * h, 4)]

            @pl.when(n < 4)
            def _(r=r, tile=tile):
                pltpu.make_async_copy(tile, a2_hbm.at[r], osem.at[0]).start()

            @pl.when(n >= 4)
            def _(r=r, tile=tile):
                pltpu.make_async_copy(tile, a1_hbm.at[r], osem.at[1]).start()

    def set_out(n):
        for turn_by in range(4):
            f = 4 * (q // 8) + turn_by
            part = obuf.at[8 * n + f]
            remote(part, part, tsend.at[n, f, 0], trecv.at[8 * n + f], p, sides[turn_by]).start()

    def forward(since, f):
        _, has, first, _ = flows[f]
        n = since - first

        @pl.when(jnp.logical_and(n >= 0, n < BLOCKS))
        def _():
            branch(n, f, 0).wait_recv()

            for e in range(4):
                @pl.when(has[e])
                def _(e=e):
                    branch(n, f, e).start()

    def chain_turn(t):
        ahead = t - 1 - HOP * pos

        @pl.when(jnp.logical_and(off_chip, jnp.logical_and(ahead >= 0, ahead < BLOCKS)))
        def _():
            chain(ahead)

    def columns(since):
        for rnd in range(2):
            @pl.when(since == COLUMN[rnd])
            def _(rnd=rnd):
                to_column(rnd)

    def pass_all(since):
        for f in range(8):
            forward(since, f)

    def produce(t, _):
        products(t)

        @pl.when(t == 3)
        def _():
            turn_panel(1)

        chain_turn(t)
        return 0

    lax.fori_loop(0, BLOCKS, produce, 0)

    def pass_sums(t, _):
        chain_turn(t)
        return 0

    lax.fori_loop(BLOCKS, START, pass_sums, 0)

    @pl.when(is_dest)
    def _():
        dacc2[...] = jnp.zeros_like(dacc2)
        dacc1[...] = jnp.zeros_like(dacc1)
        for panel in range(2):
            def turn_h(col, _, panel=panel):
                load_h(panel, col).wait()
                hbuf[panel, col] = hbuf[panel, col].T
                return 0

            lax.fori_loop(0, 4, turn_h, 0)
        keep_turned(0, w2_ref[...])
        keep_turned(1, w1_ref[...])
        corner_here.wait()
        keep_turned(2, kbuf[...])

    def finish_step(since, _):
        chain_turn(START + since)

        @pl.when(is_dest)
        def _():
            @pl.when(since < 4)
            def _():
                finish_two(since)

            @pl.when(since >= 4)
            def _():
                finish_one(since)

            set_out(since)

        pass_all(since)

        @pl.when(is_dest)
        def _():
            @pl.when(since < 4)
            def _():
                sums_two(since)

            @pl.when(since >= 4)
            def _():
                sums_one(since)

            for rnd in range(2):
                @pl.when(since == SPREAD[rnd])
                def _(rnd=rnd):
                    spread_all(rnd)

            @pl.when(since == OWN[0])
            def _():
                own_rows(0)

        return 0

    lax.fori_loop(0, BLOCKS, finish_step, 0)

    def last_step(since, _):
        pass_all(since)

        @pl.when(jnp.logical_and(is_dest, since == OWN[1]))
        def _():
            own_rows(1)

        columns(since)
        complete = since - TREE * DEEPEST

        @pl.when(complete >= 0)
        def _():
            store(complete)

        return 0

    lax.fori_loop(BLOCKS, LAST + 1, last_step, 0)

    for rnd, out in ((0, d2_hbm), (1, d1_hbm)):
        def late(i, _, rnd=rnd):
            pair_rows(rnd, (p + i) % 8, 0).wait_recv()
            return 0

        lax.fori_loop(1, 8, late, 0)
        pltpu.make_async_copy(dfull.at[rnd], out, osem.at[2 + rnd]).start()

    def sent(n, _):
        @pl.when(helper)
        def _():
            swap_whole(n).wait_send()

        @pl.when(off_chip)
        def _():
            swap_half(n).wait_send()
            pass_on(n).wait_send()

        return 0

    lax.fori_loop(0, BLOCKS, sent, 0)

    @pl.when(jnp.logical_and(p == 0, jnp.logical_not(is_dest)))
    def _():
        corner.wait_send()

    for f in range(8):
        for e in range(4):
            @pl.when(flows[f][1][e])
            def _(f=f, e=e):
                def part_sent(n, _):
                    branch(n, f, e).wait_send()
                    return 0

                lax.fori_loop(0, BLOCKS, part_sent, 0)

    for rnd in range(2):
        def column_sent(i, _, rnd=rnd):
            pair_rows(rnd, p, i).wait_send()
            return 0

        lax.fori_loop(1, 8, column_sent, 0)

        @pl.when(is_dest)
        def _(rnd=rnd):
            def home_sent(i, _):
                spread(rnd, (q + i) % 16, q).wait_send()
                to_plane(rnd, i, q // 8).wait_send()
                return 0

            lax.fori_loop(1, 16, home_sent, 0)

    @pl.when(jnp.logical_and(is_dest, jnp.logical_not(is_root)))
    def _():
        cross_rows(q).wait_send()

    pltpu.make_async_copy(a2_hbm, a2_hbm, osem.at[0]).wait()
    pltpu.make_async_copy(a1_hbm, a1_hbm, osem.at[1]).wait()
    pltpu.make_async_copy(dfull.at[0], d2_hbm, osem.at[2]).wait()
    pltpu.make_async_copy(dfull.at[1], d1_hbm, osem.at[3]).wait()


def hand_over(a1_in, a2_in, d1_in, d2_in, a1_out, a2_out, d1_out, d2_out, tiles, squares, sem_in, sem_out):
    moves = []
    for r in range(8):
        moves.append((a1_in.at[r, 0], tiles.at[0, r], a1_out.at[r, 0]))
        moves.append((a2_in.at[r, 0], tiles.at[1, r], a2_out.at[r, 0]))
    moves.append((d1_in, squares.at[0], d1_out))
    moves.append((d2_in, squares.at[1], d2_out))
    loads = [pltpu.make_async_copy(src, mid, sem_in.at[i]) for i, (src, mid, _) in enumerate(moves)]
    stores = [pltpu.make_async_copy(mid, dst, sem_out.at[i]) for i, (_, mid, dst) in enumerate(moves)]
    for load in loads:
        load.start()
    for load, store in zip(loads, stores):
        load.wait()
        store.start()
    for store in stores:
        store.wait()


def local(grad_trailing, panel_one, panel_two, grad_one, grad_two, inv_one, inv_two):
    any_space = pl.BlockSpec(memory_space=pl.ANY)
    vmem = pl.BlockSpec(memory_space=pltpu.VMEM)
    panel = jax.ShapeDtypeStruct(panel_one.shape, F32)
    grouped = jax.ShapeDtypeStruct((8, 4, QUARTER, B), F32)
    square = jax.ShapeDtypeStruct((B, B), F32)
    dma = pltpu.SemaphoreType.DMA
    results = pl.pallas_call(
        kernel,
        out_shape=(grouped, grouped, square, square),
        in_specs=[any_space] * 5 + [vmem] * 2,
        out_specs=(any_space,) * 4,
        scratch_shapes=[
            pltpu.VMEM((4, 8, B, B), F32),
            pltpu.VMEM((4, 8 * B, B), BF16),
            pltpu.VMEM((4, 8 * B, B), BF16),
            pltpu.VMEM((3, B, B), BF16),
            pltpu.VMEM((3, B, B), BF16),
            pltpu.VMEM((2, 8, B, B), F32),
            pltpu.VMEM((2 * B, 8 * B), BF16),
            pltpu.VMEM((2 * B, 8 * B), BF16),
            pltpu.VMEM((2, 4, B, B), F32),
            pltpu.VMEM((B, B), F32),
            pltpu.VMEM((4, B, B), F32),
            pltpu.VMEM((BLOCKS, B, B), F32),
            pltpu.VMEM((BLOCKS, B, B), F32),
            pltpu.VMEM((BLOCKS, 2, HALF, B), F32),
            pltpu.VMEM((BLOCKS, HALF, B), F32),
            pltpu.VMEM((8 * BLOCKS, QUARTER, B), F32),
            pltpu.VMEM((BLOCKS, B, B), F32),
            pltpu.VMEM((16, 32, B), F32),
            pltpu.VMEM((16, 16, B), F32),
            pltpu.VMEM((16, 32, B), F32),
            pltpu.VMEM((16, 16, B), F32),
            pltpu.VMEM((2, B, B), F32),
            pltpu.VMEM((B, B), F32),
            dma((4,)),
            dma((2,)),
            dma((2, 4)),
            dma,
            dma,
            dma((BLOCKS,)),
            dma((BLOCKS,)),
            dma((BLOCKS,)),
            dma((BLOCKS, 2)),
            dma((BLOCKS, 8, 4)),
            dma((BLOCKS * 8,)),
            dma((4,)),
            dma((2, 16)),
            dma((2, 16)),
            dma((2, 16)),
            dma((2, 2)),
            dma((2, 8)),
            dma((2, 8)),
            dma,
            dma((16,)),
        ],
        compiler_params=pltpu.CompilerParams(
            collective_id=0, has_side_effects=True, vmem_limit_bytes=56 * 2**20
        ),
        cost_estimate=pl.CostEstimate(flops=7_000_000_000, bytes_accessed=22_000_000, transcendentals=0),
    )(grad_trailing, panel_one, panel_two, grad_one, grad_two, inv_one, inv_two)
    return pl.pallas_call(
        hand_over,
        out_shape=(panel, panel, square, square),
        in_specs=[any_space] * 4,
        out_specs=(any_space,) * 4,
        scratch_shapes=[
            pltpu.VMEM((2, 8, B, B), F32),
            pltpu.VMEM((2, B, B), F32),
            dma((18,)),
            dma((18,)),
        ],
        compiler_params=pltpu.CompilerParams(vmem_limit_bytes=16 * 2**20),
    )(results[0].reshape(panel.shape), results[1].reshape(panel.shape), *results[2:])


def solution(mesh):
    placed = (
        P(None, "prow", None, None, "pcol", None),
        P(None, "prow", None, None),
        P(None, "prow", None, None),
        P(None, "prow", None, None),
        P(None, "prow", None, None),
        P(),
        P(),
    )
    return jax.shard_map(
        local,
        mesh=mesh,
        in_specs=placed,
        out_specs=(P(None, "prow", None, None), P(None, "prow", None, None), P(), P()),
        check_vma=False,
    )
```
